256 devices in a mesh: dp: 32 (over z_lo, x, core), tensor: 8 (over y, z_hi).
Axes of the slice: x: 4, y: 4, z: 8 (z_hi: 2, z_lo: 4; z = z_hi * 4 + z_lo), core: 2. Of those that a mesh axis runs over, the one named last changes fastest.
Arguments:
- tokens: bfloat16 [8192, 4096], P('dp', 'tensor'), may hold values from -6 to 6
- doc_ids: int32 [32, 256], P('dp'), may hold values from 0 to 31, never falling along the last dimension, each value on 1 to 64 neighbouring positions
- wq: bfloat16 [4096, 4096], P(None, 'tensor')
- wkv: bfloat16 [4096, 2, 1024], P(None, None, 'tensor')
- wo: bfloat16 [4096, 4096], P('tensor'), may hold values from -0.09375 to 0.09375
- gate_blocks: bfloat16 [32, 8, 6, 128, 128], P('dp', 'tensor'), may hold values from -0.15625 to 0.15625
- up_blocks: bfloat16 [32, 8, 6, 128, 128], P('dp', 'tensor'), may hold values from -0.15625 to 0.15625
- keep_mask: int32 [2, 32, 112], replicated, may hold values from 0 to 1, as said below
- owner_map: int32 [2, 32, 112], replicated, may hold values from 0 to 31, as said below
- hidden_cot: bfloat16 [8192, 14336], P('dp', 'tensor'), may hold values from -0.75 to 0.75
Outputs:
- mixed: bfloat16 [8192, 4096], P('dp', 'tensor')
- hidden: bfloat16 [8192, 14336], P('dp', 'tensor')
- gate_grad: float32 [32, 8, 6, 128, 128], P('dp', 'tensor')
- up_grad: float32 [32, 8, 6, 128, 128], P('dp', 'tensor')
The draws below stay inside these ranges and needn't reach their ends.
Inputs may be any that keep to these rules, and one draw needn't show every extreme that they name: `keep_mask`: in each matrix and each column group of 14 block columns starting at a multiple of 14, exactly 134 blocks are kept. `owner_map`: among the kept blocks of one matrix and one column group, at most 6 have the same owner, and some owner has exactly 6. Values at blocks that are not kept have no meaning.
All inputs are finite; a program needn't handle non-finite values.
Results may differ from the reference program's by a relative error of at most 0.04.
Values may be sent and summed in bfloat16 or wider, within the bound.
No kernel may reach another device: no remote copies, remote signals or barrier semaphores. Data moves between devices by JAX's collectives and lax.ppermute only.
A program may use at most 192 MiB of HBM per device.

```python
import math
import jax
import jax.numpy as jnp
import numpy as np
from jax import lax

D = 4096
FF = 14336
HEADS = 32
KV_HEADS = 8
HEAD_DIM = 128
BLK = 128
SEQ = 256
KB_D = 32
KB_F = 112
KBF_T = 14
CAP = 6
KEEP = 134
PACKS = 32
TOKENS = 8192
N_DP = 32
N_TENSOR = 8


def blocks_layout(key):
    groups = 2 * N_TENSOR
    count = KB_D * KBF_T
    slots = N_DP * CAP
    keys = jax.random.split(key, 4)
    scores = jax.vmap(lambda sub_key: jax.random.permutation(sub_key, count))(jax.random.split(keys[0], groups))
    kept = (scores.astype(jnp.int32) < KEEP).astype(jnp.int32)
    kept_rank = jnp.maximum(jnp.cumsum(kept, axis=1) - 1, 0)
    heavy = jax.random.randint(keys[1], (groups, 1), 0, N_DP)
    slot_owner = jnp.arange(slots, dtype=jnp.int32)[None, :] // CAP
    order_scores = jax.vmap(lambda sub_key: jax.random.permutation(sub_key, slots))(jax.random.split(keys[2], groups))
    order_scores = order_scores.astype(jnp.int32) - slots * (slot_owner == heavy).astype(jnp.int32)
    order = jnp.argsort(order_scores, axis=1, stable=True).astype(jnp.int32)
    chosen = jnp.take_along_axis(order, kept_rank, axis=1)
    filler = jax.random.randint(keys[3], (groups, count), 0, N_DP)
    owner = jnp.where(kept == 1, chosen // CAP, filler).astype(jnp.int32)

    def arrange(table):
        return table.reshape(2, N_TENSOR, KB_D, KBF_T).transpose(0, 2, 1, 3).reshape(2, KB_D, KB_F)
    return (arrange(kept), arrange(owner))


def draw_keep_mask(key, part):
    return blocks_layout(key)[0]


def draw_owner_map(key, part):
    return blocks_layout(key)[1]


def shared_keys(key):
    return jax.random.normal(key, (D, KV_HEADS * HEAD_DIM), jnp.float32)


def draw_wkv(key, part):
    base = shared_keys(key)
    key = jax.random.fold_in(key, 11)
    values_part = jax.random.normal(key, (D, KV_HEADS * HEAD_DIM), jnp.float32)
    return (jnp.stack([base, values_part], axis=1) * D ** (-0.5)).astype(jnp.bfloat16)


def draw_wq(key, part):
    key = jax.random.fold_in(key, 12)
    noise = jax.random.normal(key, (D, HEADS * HEAD_DIM), jnp.float32)
    return (noise * D ** (-0.5)).astype(jnp.bfloat16)


def block_scale(stream_key, dims, cuts, low, high):
    def one(axis_at, parts):
        draws = jax.random.uniform(jax.random.fold_in(jax.random.fold_in(stream_key, 6), axis_at), (parts,), jnp.float32, low / len(cuts), high / len(cuts))
        return jnp.repeat(jnp.exp(draws), dims[axis_at] // parts).reshape((-1,) + (1,) * (len(dims) - axis_at - 1))

    factor_of = one(*cuts[0])
    for cut in cuts[1:]:
        factor_of = factor_of * one(*cut)
    return factor_of


def split_up(amount, total, limit, slope):
    portions = [(1 << 20) // math.isqrt(standing ** slope) + 1 for standing in range(2, amount + 1)]
    surplus, counts = total - limit - (amount - 1), [1] * (amount - 1)
    while surplus > 0:
        free = [i for i in range(amount - 1) if counts[i] < limit]
        whole, remaining = sum([portions[i] for i in free]), surplus
        for i in free:
            extra = min(limit - counts[i], max(1, remaining * portions[i] // whole), surplus)
            counts[i] = counts[i] + extra
            surplus = surplus - extra
    return np.array([limit] + counts)


def ragged(own_key, number_of, total, bound, skew):
    if number_of == 2:
        one = jax.random.randint(own_key, (), max(1, total - bound), min(bound, total - 1) + 1)
        return jnp.stack([one, total - one])
    tallies = jnp.asarray(split_up(number_of, total, bound, skew), jnp.int32)
    pairs = (number_of - 1) // 2
    source_of, taker = tallies[1:1 + 2 * pairs:2], tallies[2:2 + 2 * pairs:2]
    room = jnp.minimum(source_of - 1, bound - taker)
    passed = jax.random.randint(jax.random.fold_in(own_key, 1), (pairs,), 0, 1 << 20) % (room + 1)
    tallies = tallies.at[1:1 + 2 * pairs:2].set(source_of - passed).at[2:2 + 2 * pairs:2].set(taker + passed)
    return tallies[jax.random.permutation(jax.random.fold_in(own_key, 2), number_of)]


def scatter_about(rng, extent, spread, most, cuts=(), kind=jnp.bfloat16):
    loudness = block_scale(rng, extent, cuts, -0.22, 0.18) if cuts else 1.0
    entries = jax.random.normal(rng, extent, jnp.float32) * spread * loudness
    return jnp.minimum(jnp.maximum(entries, -most), most).astype(kind)


def setup_inputs(seed: int = 0) -> dict:
    splits = jax.random.split(jax.random.key(seed), 11)
    return {
        "tokens": scatter_about(splits[0], (TOKENS, D), 1.0, 6.0, ((0, 32), (1, 8))),
        "doc_ids": jax.vmap(lambda own: jnp.searchsorted(jnp.cumsum(ragged(own, SEQ // 8, SEQ, max(SEQ // 4, 16), 2)), jnp.arange(SEQ), side="right"))(jax.random.split(splits[1], PACKS)).reshape((PACKS, SEQ)).astype(jnp.int32),
        "wq": draw_wq(jax.random.fold_in(splits[10], 71), 0),
        "wkv": draw_wkv(jax.random.fold_in(splits[10], 71), 0),
        "wo": scatter_about(splits[4], (HEADS * HEAD_DIM, D), (HEADS * HEAD_DIM) ** -0.5, 0.09375, ((0, 8),)),
        "gate_blocks": scatter_about(splits[5], (N_DP, N_TENSOR, CAP, BLK, BLK), (3 * D // 10) ** -0.5, 0.15625, ((0, 32), (1, 8))),
        "up_blocks": scatter_about(splits[6], (N_DP, N_TENSOR, CAP, BLK, BLK), (3 * D // 10) ** -0.5, 0.15625, ((0, 32), (1, 8))),
        "keep_mask": draw_keep_mask(jax.random.fold_in(splits[10], 71), 0),
        "owner_map": draw_owner_map(jax.random.fold_in(splits[10], 71), 0),
        "hidden_cot": scatter_about(splits[9], (TOKENS, FF), 0.05, 0.75, ((0, 32), (1, 8))),
    }


EPS = 1e-05
THETA = 10000.0

def rms_scale(values):
    return lax.rsqrt(lax.optimization_barrier(jnp.mean(values * values, axis=-1, keepdims=True)) + EPS)

def rotate(heads, positions):
    half_dim = heads.shape[-1] // 2
    freqs = jnp.exp(-jnp.log(THETA) * jnp.arange(half_dim, dtype=jnp.float32) * 2.0 / heads.shape[-1])
    angles = positions[:, None] * freqs[None, :]
    cosine = jnp.cos(angles)[:, None, :]
    sine = jnp.sin(angles)[:, None, :]
    first = heads[..., :half_dim]
    second = heads[..., half_dim:]
    return jnp.concatenate([first * cosine - second * sine, second * cosine + first * sine], axis=-1)

def attention(x_pack, docs, wq, wkv, wo):
    rows_len = x_pack.shape[0]
    x_wide = x_pack.astype(jnp.float32)
    normed = (x_wide * rms_scale(x_wide)).astype(jnp.bfloat16)
    positions = jnp.arange(rows_len, dtype=jnp.float32)
    queries = jnp.dot(normed, wq, preferred_element_type=jnp.float32).reshape(rows_len, HEADS, HEAD_DIM)
    key_vals = jnp.dot(normed, wkv.reshape(D, 2 * KV_HEADS * HEAD_DIM), preferred_element_type=jnp.float32)
    key_vals = key_vals.reshape(rows_len, 2, KV_HEADS, HEAD_DIM)
    queries = rotate(queries, positions).astype(jnp.bfloat16).reshape(rows_len, KV_HEADS, HEADS // KV_HEADS, HEAD_DIM)
    keys_rot = rotate(key_vals[:, 0], positions).astype(jnp.bfloat16)
    values_v = key_vals[:, 1].astype(jnp.bfloat16)
    scores = jnp.einsum('qhgd,khd->hgqk', queries.astype(jnp.float32), keys_rot.astype(jnp.float32)) * HEAD_DIM ** (-0.5)
    places = jnp.arange(rows_len)
    allowed = (docs[:, None] == docs[None, :]) & (places[None, :] <= places[:, None])
    scores = jnp.where(allowed, scores, -1e+30)
    highest = lax.optimization_barrier(jnp.max(scores, axis=-1, keepdims=True))
    weights = jnp.exp(scores - highest)
    probs = (weights / lax.optimization_barrier(jnp.sum(weights, axis=-1, keepdims=True))).astype(jnp.bfloat16)
    context = jnp.einsum('hgqk,khd->qhgd', probs.astype(jnp.float32), values_v.astype(jnp.float32))
    context = context.astype(jnp.bfloat16).reshape(rows_len, HEADS * HEAD_DIM)
    return jnp.dot(context, wo, preferred_element_type=jnp.float32)

def kept_layout(keep, owner, group):
    kept = keep[:, group * KBF_T:(group + 1) * KBF_T].reshape(-1)
    owners = owner[:, group * KBF_T:(group + 1) * KBF_T].reshape(-1)
    member = ((owners[:, None] == jnp.arange(N_DP, dtype=jnp.int32)[None, :]) & (kept[:, None] == 1)).astype(jnp.int32)
    ranks = lax.optimization_barrier(jnp.sum(member * (jnp.cumsum(member, axis=0) - 1), axis=1))
    slots = owners * CAP + ranks
    listed = jnp.argsort(1 - kept, stable=True)[:KEEP].astype(jnp.int32)
    return (listed // KBF_T, listed % KBF_T, slots[listed])

def reference(tokens, doc_ids, wq, wkv, wo, gate_blocks, up_blocks, keep_mask, owner_map, hidden_cot):
    layouts = []
    for matrix_index, stored_blocks in enumerate((gate_blocks, up_blocks)):
        per_group = []
        for group in range(N_TENSOR):
            rows_idx, cols_idx, slot_idx = kept_layout(keep_mask[matrix_index], owner_map[matrix_index], group)
            stored = stored_blocks[:, group].reshape(N_DP * CAP, BLK, BLK)[slot_idx]
            per_group.append((rows_idx, cols_idx, slot_idx, stored))
        layouts.append(per_group)

    def one_pack(totals, item):
        x_pack, docs, cot_pack = item
        resid = x_pack.astype(jnp.float32) + attention(x_pack, docs, wq, wkv, wo)
        normed = (resid * rms_scale(resid)).astype(jnp.bfloat16)
        x_blocks = normed.reshape(SEQ, KB_D, BLK).astype(jnp.float32)
        pre_acts = []
        for per_group in layouts:
            columns = []
            for rows_idx, cols_idx, slot_idx, stored in per_group:
                products = jnp.einsum('tsk,skn->tsn', x_blocks[:, rows_idx], stored.astype(jnp.float32))
                placed = jnp.zeros((SEQ, KBF_T, BLK), jnp.float32).at[:, cols_idx].add(products)
                columns.append(placed.reshape(SEQ, KBF_T * BLK))
            pre_acts.append(jnp.concatenate(columns, axis=1))
        gate, upper = pre_acts
        sigma = jax.nn.sigmoid(gate)
        activ = gate * sigma
        hidden = (activ * upper).astype(jnp.bfloat16)
        cot_wide = cot_pack.astype(jnp.float32)
        d_gate = (cot_wide * upper * sigma * (1.0 + gate * (1.0 - sigma))).astype(jnp.bfloat16)
        d_up = (cot_wide * activ).astype(jnp.bfloat16)
        new_totals = []
        for total, per_group, grads_in in zip(totals, layouts, (d_gate, d_up)):
            grad_blocks = grads_in.reshape(SEQ, N_TENSOR, KBF_T, BLK).astype(jnp.float32)
            updated = []
            for group_index, (rows_idx, cols_idx, slot_idx, stored) in enumerate(per_group):
                partial_grad = jnp.einsum('tsk,tsn->skn', x_blocks[:, rows_idx], grad_blocks[:, group_index][:, cols_idx])
                rounded = lax.optimization_barrier(partial_grad.astype(jnp.bfloat16)).astype(jnp.float32)
                updated.append(total[group_index] + rounded)
            new_totals.append(jnp.stack(updated))
        return ((new_totals[0], new_totals[1]), (resid.astype(jnp.bfloat16), hidden))
    zero_sums = jnp.zeros((N_TENSOR, KEEP, BLK, BLK), jnp.float32)
    items = (tokens.reshape(N_DP, SEQ, D), doc_ids, hidden_cot.reshape(N_DP, SEQ, FF))
    totals, (mixed, hidden) = lax.scan(one_pack, (zero_sums, zero_sums), items)
    grads_out = []
    for total, per_group in zip(totals, layouts):
        placed_groups = []
        for group_index, (rows_idx, cols_idx, slot_idx, stored) in enumerate(per_group):
            flat = jnp.zeros((N_DP * CAP, BLK, BLK), jnp.float32).at[slot_idx].set(total[group_index])
            placed_groups.append(flat.reshape(N_DP, CAP, BLK, BLK))
        grads_out.append(jnp.stack(placed_groups, axis=1))
    return (mixed.reshape(TOKENS, D), hidden.reshape(TOKENS, FF), grads_out[0], grads_out[1])
```

```python
import jax
import jax.numpy as jnp
from jax import lax
from jax.experimental import pallas as pl
from jax.experimental.pallas import tpu as pltpu
from jax.sharding import PartitionSpec as P

HEAD_DIM = 128
BLK = 128
EPS = 1e-05
THETA = 10000.0
NZ, NX, NC = 4, 4, 2
NY, NH = 4, 2
STATIC = 12
EXTRA = 4
MIB = 1024 * 1024

SMEM = pl.BlockSpec(memory_space=pltpu.SMEM)
VMEM = pl.BlockSpec(memory_space=pltpu.VMEM)
ANY = pl.BlockSpec(memory_space=pl.ANY)


def dp_perm(dz, dx, dc):
    pairs = []
    for z in range(NZ):
        for x in range(NX):
            for c in range(NC):
                src = (z * NX + x) * NC + c
                dst = (((z + dz) % NZ) * NX + (x + dx) % NX) * NC + (c + dc) % NC
                pairs.append((src, dst))
    return pairs


def send_dp(value, dz, dx, dc):
    return lax.ppermute(value, "dp", dp_perm(dz, dx, dc))


def send_tensor(value, dy, dh):
    pairs = []
    for y in range(NY):
        for h in range(NH):
            pairs.append((y * NH + h, ((y + dy) % NY) * NH + (h + dh) % NH))
    return lax.ppermute(value, "tensor", pairs)


def rope_tables(rows_len):
    half_dim = HEAD_DIM // 2
    positions = jnp.arange(rows_len, dtype=jnp.float32)
    freqs = jnp.exp(
        -jnp.log(THETA) * jnp.arange(half_dim, dtype=jnp.float32) * 2.0 / HEAD_DIM
    )
    angles = positions[:, None] * freqs[None, :]
    cosine = jnp.cos(angles)
    sine = jnp.sin(angles)
    return jnp.concatenate([cosine, cosine], 1), jnp.concatenate([-sine, sine], 1)


def block_tables(keep, owner, group, width, capacity):
    dp_index = lax.axis_index("dp")
    my_c = dp_index % NC
    my_x = (dp_index // NC) % NX
    my_z = dp_index // (NC * NX)
    rows_count = keep.shape[0]
    kept = lax.dynamic_slice_in_dim(keep, group * width, width, 1)
    owners = lax.dynamic_slice_in_dim(owner, group * width, width, 1)
    flat_kept = kept.reshape(-1)
    flat_owner = owners.reshape(-1)
    count = flat_kept.shape[0]
    order = jnp.arange(count, dtype=jnp.int32)
    same = (
        (flat_owner[:, None] == flat_owner[None, :])
        & (order[None, :] < order[:, None])
        & (flat_kept[None, :] == 1)
    )
    ranks = jnp.sum(same.astype(jnp.int32), axis=1)
    rel_c = (flat_owner + my_c) % NC
    rel_x = (flat_owner // NC + NX - my_x) % NX
    rel_z = (flat_owner // (NC * NX) + NZ - my_z) % NZ
    places = ((rel_c * NX + rel_x) * NZ + rel_z) * capacity + ranks
    slots = NC * NX * NZ * capacity
    places = jnp.where(flat_kept == 1, places, slots)
    hits = places[:, None] == jnp.arange(slots, dtype=jnp.int32)[None, :]
    code = jnp.sum(jnp.where(hits, order[:, None] + 1, 0), axis=0) - 1
    slot_row = jnp.where(code >= 0, code // width, 0)
    slot_col = jnp.where(code >= 0, code % width, -1)
    grid_places = places.reshape(rows_count, width)
    below = jnp.cumsum(kept, axis=0) - kept
    wanted = (below[:, :, None] == jnp.arange(rows_count, dtype=jnp.int32)[None, None, :]) & (
        kept[:, :, None] == 1
    )
    rows = jnp.arange(rows_count, dtype=jnp.int32)[:, None, None]
    list_row = jnp.sum(jnp.where(wanted, rows, 0), axis=0)
    list_place = slots + jnp.sum(jnp.where(wanted, grid_places[:, :, None] - slots, 0), axis=0)
    col_count = jnp.sum(kept, axis=0)
    return slot_row, slot_col, list_row, list_place, col_count


def attention_kernel(*refs):
    index_ref = refs[0]
    pieces = refs[1:9]
    wq_ref, wkv_ref, wo_ref, cos_ref, sin_ref, drow_ref, dcol_ref = refs[9:16]
    outs = refs[16:24]
    rows_len, share = pieces[0].shape
    width = share * len(pieces)
    q_acc = jnp.zeros((rows_len, wq_ref.shape[1]), jnp.float32)
    kv_acc = jnp.zeros((rows_len, wkv_ref.shape[1]), jnp.float32)
    squares = jnp.zeros((rows_len, 1), jnp.float32)
    for i, piece in enumerate(pieces):
        at = pl.multiple_of(index_ref[i] * share, share)
        x = piece[...]
        q_acc += jnp.dot(x, wq_ref[pl.ds(at, share), :], preferred_element_type=jnp.float32)
        kv_acc += jnp.dot(x, wkv_ref[pl.ds(at, share), :], preferred_element_type=jnp.float32)
        wide = x.astype(jnp.float32)
        squares += jnp.sum(wide * wide, axis=1, keepdims=True)
    scale = lax.rsqrt(squares / width + EPS)
    cosine = cos_ref[...]
    sine = sin_ref[...]

    def rotated(raw):
        normed = raw * scale
        return (normed * cosine + pltpu.roll(normed, HEAD_DIM // 2, 1) * sine).astype(jnp.bfloat16)

    key = rotated(kv_acc[:, :HEAD_DIM])
    value = (kv_acc[:, HEAD_DIM:] * scale).astype(jnp.bfloat16)
    q_pos = lax.broadcasted_iota(jnp.int32, (rows_len, rows_len), 0)
    k_pos = lax.broadcasted_iota(jnp.int32, (rows_len, rows_len), 1)
    allowed = (drow_ref[...] == dcol_ref[...]) & (k_pos <= q_pos)
    contexts = []
    for head in range(wq_ref.shape[1] // HEAD_DIM):
        query = rotated(q_acc[:, head * HEAD_DIM : (head + 1) * HEAD_DIM])
        scores = lax.dot_general(
            query, key, (((1,), (1,)), ((), ())), preferred_element_type=jnp.float32
        ) * (HEAD_DIM ** (-0.5))
        scores = jnp.where(allowed, scores, -1e30)
        highest = jnp.max(scores, axis=1, keepdims=True)
        weights = jnp.exp(scores - highest)
        probs = (weights / jnp.sum(weights, axis=1, keepdims=True)).astype(jnp.bfloat16)
        contexts.append(
            jnp.dot(probs, value, preferred_element_type=jnp.float32).astype(jnp.bfloat16)
        )
    context = jnp.concatenate(contexts, axis=1)
    for i, out in enumerate(outs):
        at = pl.multiple_of(index_ref[i] * share, share)
        out[...] = jnp.dot(
            context, wo_ref[:, pl.ds(at, share)], preferred_element_type=jnp.float32
        ).astype(jnp.bfloat16)


def forward_kernel(n_weights, *refs):
    index_ref, row_ref, place_ref, count_ref = refs[:4]
    pieces = refs[4:12]
    weights = refs[12 : 12 + n_weights]
    cot_ref = refs[12 + n_weights]
    hidden_ref, dgate_ref, dup_ref, xt_ref = refs[13 + n_weights : 17 + n_weights]
    w_ref, xb_ref, sem = refs[17 + n_weights :]
    rows_len, share = pieces[0].shape
    per_piece = share // BLK
    model_width = share * len(pieces)
    slots = w_ref.shape[1] - 1

    copies = []
    for i, weight in enumerate(weights):
        matrix, start = divmod(i, n_weights // 2)
        size = weight.shape[0]
        begin = sum(w.shape[0] for w in weights[:start])
        copies.append(
            pltpu.make_async_copy(weight, w_ref.at[matrix, pl.ds(begin, size)], sem.at[i])
        )
    for copy in copies:
        copy.start()
    squares = jnp.zeros((rows_len, 1), jnp.float32)
    for i, piece in enumerate(pieces):
        x = piece[...]
        wide = x.astype(jnp.float32)
        squares += jnp.sum(wide * wide, axis=1, keepdims=True)
        for q in range(per_piece):
            block = x[:, q * BLK : (q + 1) * BLK]
            xb_ref[index_ref[i] * per_piece + q] = block
            xt_ref[index_ref[i] * per_piece + q] = block.T
    scale = lax.rsqrt(squares / model_width + EPS)
    for matrix in range(2):
        w_ref[matrix, slots] = jnp.zeros((BLK, BLK), jnp.bfloat16)
    for copy in copies:
        copy.wait()

    def product(matrix, col, first, amount):
        x = [xb_ref[row_ref[matrix, col, first + k]] for k in range(amount)]
        w = [w_ref[matrix, place_ref[matrix, col, first + k]] for k in range(amount)]
        return jnp.dot(
            jnp.concatenate(x, 1), jnp.concatenate(w, 0), preferred_element_type=jnp.float32
        )

    def column(col, carry):
        sums = []
        for matrix in range(2):
            total = product(matrix, col, 0, STATIC)
            more = (jnp.maximum(count_ref[matrix, col] - STATIC, 0) + EXTRA - 1) // EXTRA

            def step(n, acc, matrix=matrix):
                return acc + product(matrix, col, STATIC + n * EXTRA, EXTRA)

            sums.append(lax.fori_loop(0, more, step, total))
        gate = sums[0] * scale
        upper = sums[1] * scale
        at = pl.ds(pl.multiple_of(col * BLK, BLK), BLK)
        cot = cot_ref[:, at].astype(jnp.float32)
        sigma = 1.0 / (1.0 + jnp.exp(-gate))
        activ = gate * sigma
        hidden_ref[:, at] = (activ * upper).astype(jnp.bfloat16)
        scaled = cot * scale
        dgate_ref[col] = (scaled * upper * sigma * (1.0 + gate * (1.0 - sigma))).astype(jnp.bfloat16)
        dup_ref[col] = (scaled * activ).astype(jnp.bfloat16)
        return carry

    lax.fori_loop(0, dgate_ref.shape[0], column, 0)


def term(xt_ref, grads_ref, row_ref, col_ref, slot):
    col = col_ref[slot]
    value = jnp.dot(
        xt_ref[row_ref[slot]], grads_ref[jnp.maximum(col, 0)], preferred_element_type=jnp.float32
    )
    return jnp.where(col >= 0, value, 0.0)


def far_kernel(first, unroll, row_ref, col_ref, xt_ref, grads_ref, out_ref):
    def step(n, carry):
        for k in range(unroll):
            slot = n * unroll + k
            out_ref[slot] = term(xt_ref, grads_ref, row_ref, col_ref, first + slot).astype(
                jnp.bfloat16
            )
        return carry

    lax.fori_loop(0, out_ref.shape[0] // unroll, step, 0)


def near_kernel(unroll, row_ref, col_ref, xt_ref, grads_ref, add_ref, *outs):
    first = 0
    for out_ref in outs:

        def step(n, carry, out_ref=out_ref, first=first):
            for k in range(unroll):
                slot = n * unroll + k
                value = term(xt_ref, grads_ref, row_ref, col_ref, first + slot)
                value += add_ref[first + slot].astype(jnp.float32)
                out_ref[slot] = value.astype(jnp.bfloat16)
            return carry

        lax.fori_loop(0, out_ref.shape[0] // unroll, step, 0)
        first += out_ref.shape[0]


def shape_of(shape, dtype=jnp.bfloat16):
    return jax.ShapeDtypeStruct(shape, dtype)


def params(mib):
    return pltpu.CompilerParams(vmem_limit_bytes=mib * MIB)


def wide_sum(*values):
    total = values[0].astype(jnp.float32)
    for value in values[1:]:
        total = total + value.astype(jnp.float32)
    return total


def gather_tensor(own):
    other = send_tensor(own, 0, 1)
    first = [own] + [send_tensor(own, d, 0) for d in (1, 3, 2)]
    second = [other] + [send_tensor(other, d, 0) for d in (1, 3, 2)]
    return first + second


def gather_blocks(own):
    along_z = jnp.concatenate(
        [own] + [send_dp(own, d, 0, 0) for d in (3, 2, 1)], axis=0
    )
    half = along_z.shape[0] // 2
    left = send_dp(along_z, 0, 1, 0)
    right = send_dp(along_z, 0, 3, 0)
    far_a = send_dp(left[:half], 0, 1, 0)
    far_b = send_dp(right[half:], 0, 3, 0)
    mine = [along_z, right, far_a, far_b, left]
    return mine + [send_dp(part, 0, 0, 1) for part in mine]


def local(tokens, doc_ids, wq, wkv, wo, gate_blocks, up_blocks, keep_mask, owner_map, hidden_cot):
    dp_unused = None
    del dp_unused
    group = lax.axis_index("tensor")
    my_y = group // NH
    my_h = group % NH
    capacity = gate_blocks.shape[2]
    rows_len, share = tokens.shape
    n_share = lax.axis_size("tensor")
    model_width = share * n_share
    width = hidden_cot.shape[1] // BLK
    bf16 = jnp.bfloat16

    got = jnp.stack(
        [((my_y + NY - d) % NY) * NH + (my_h + h) % NH for h in range(NH) for d in (0, 1, 3, 2)]
    ).astype(jnp.int32)
    sent = jnp.stack(
        [((my_y + d) % NY) * NH + (my_h + h) % NH for h in range(NH) for d in (0, 3, 1, 2)]
    ).astype(jnp.int32)

    pieces = gather_tensor(tokens)
    gate_parts = gather_blocks(gate_blocks.reshape(capacity, BLK, BLK))
    up_parts = gather_blocks(up_blocks.reshape(capacity, BLK, BLK))

    cosine, sine = rope_tables(rows_len)
    tables = [
        block_tables(keep_mask[m], owner_map[m], group, width, capacity) for m in range(2)
    ]
    list_row = jnp.stack([t[2] for t in tables])
    list_place = jnp.stack([t[3] for t in tables])
    col_count = jnp.stack([t[4] for t in tables])

    partial = pl.pallas_call(
        attention_kernel,
        out_shape=[shape_of((rows_len, share))] * n_share,
        in_specs=[SMEM] + [VMEM] * 15,
        out_specs=[VMEM] * n_share,
        compiler_params=params(48),
        name="attention",
    )(
        sent,
        *pieces,
        wq,
        wkv.reshape(model_width, -1),
        wo,
        cosine,
        sine,
        doc_ids.reshape(rows_len, 1),
        doc_ids.reshape(1, rows_len),
    )
    crossed = wide_sum(
        partial[4],
        send_tensor(partial[5], 3, 0),
        send_tensor(partial[6], 1, 0),
        send_tensor(partial[7], 2, 0),
    ).astype(bf16)
    resid = wide_sum(
        tokens,
        partial[0],
        send_tensor(partial[1], 3, 0),
        send_tensor(partial[2], 1, 0),
        send_tensor(partial[3], 2, 0),
        send_tensor(crossed, 0, 1),
    )
    mixed = resid.astype(bf16)
    mid = gather_tensor(mixed)

    parts = gate_parts + up_parts
    slots = NC * NX * NZ * capacity
    kernel = lambda *refs: forward_kernel(len(parts), *refs)
    hidden, d_gate, d_up, x_t = pl.pallas_call(
        kernel,
        out_shape=[
            shape_of((rows_len, width * BLK)),
            shape_of((width, rows_len, BLK)),
            shape_of((width, rows_len, BLK)),
            shape_of((model_width // BLK, BLK, rows_len)),
        ],
        in_specs=[SMEM] * 4 + [VMEM] * 8 + [ANY] * len(parts) + [VMEM],
        out_specs=[VMEM] * 4,
        scratch_shapes=[
            pltpu.VMEM((2, slots + 1, BLK, BLK), bf16),
            pltpu.VMEM((model_width // BLK, rows_len, BLK), bf16),
            pltpu.SemaphoreType.DMA((len(parts),)),
        ],
        compiler_params=params(48),
        name="forward",
    )(got, list_row, list_place, col_count, *mid, *parts, hidden_cot)

    side = slots // NC
    quarter = side // NX
    half = quarter // 2

    def far(m, grads):
        kernel = lambda *refs: far_kernel(side, 6, *refs)
        return pl.pallas_call(
            kernel,
            out_shape=shape_of((side, BLK, BLK)),
            in_specs=[SMEM] * 2 + [VMEM] * 2,
            out_specs=VMEM,
            compiler_params=params(32),
            name="far",
        )(tables[m][0], tables[m][1], x_t, grads)

    def near(m, grads, add):
        kernel = lambda *refs: near_kernel(6, *refs)
        sizes = [quarter] + [half] * 6
        return pl.pallas_call(
            kernel,
            out_shape=[shape_of((size, BLK, BLK)) for size in sizes],
            in_specs=[SMEM] * 2 + [VMEM] * 3,
            out_specs=[VMEM] * len(sizes),
            compiler_params=params(32),
            name="near",
        )(tables[m][0], tables[m][1], x_t, grads, add)

    def reduce_rest(sums):
        s0, s1a, s1b, s2a, s2b, s3a, s3b = sums
        via_a = send_dp(s2a, 0, 1, 0)
        via_b = send_dp(s2b, 0, 3, 0)
        from_left_b = send_dp(s1b, 0, 1, 0)
        from_right_a = send_dp(s3a, 0, 3, 0)
        from_left_a = send_dp(wide_sum(s1a, via_a).astype(bf16), 0, 1, 0)
        from_right_b = send_dp(wide_sum(s3b, via_b).astype(bf16), 0, 3, 0)
        sum_a = wide_sum(s0[:half], from_left_a, from_right_a)
        sum_b = wide_sum(s0[half:], from_left_b, from_right_b)
        by_z = [sum_a[:capacity], sum_a[capacity:], sum_b[:capacity], sum_b[capacity:]]
        total = wide_sum(by_z[0], *[send_dp(by_z[d].astype(bf16), d, 0, 0) for d in (1, 2, 3)])
        return total.reshape(1, 1, capacity, BLK, BLK)

    far_gate = far(0, d_gate)
    swap_gate = send_dp(far_gate, 0, 0, 1)
    far_up = far(1, d_up)
    swap_up = send_dp(far_up, 0, 0, 1)
    gate_grad = reduce_rest(near(0, d_gate, swap_gate))
    up_grad = reduce_rest(near(1, d_up, swap_up))
    return (mixed, hidden, gate_grad, up_grad)


def solution(mesh):
    in_specs = (
        P("dp", "tensor"),
        P("dp", None),
        P(None, "tensor"),
        P(None, None, "tensor"),
        P("tensor", None),
        P("dp", "tensor", None, None, None),
        P("dp", "tensor", None, None, None),
        P(),
        P(),
        P("dp", "tensor"),
    )
    out_specs = (
        P("dp", "tensor"),
        P("dp", "tensor"),
        P("dp", "tensor", None, None, None),
        P("dp", "tensor", None, None, None),
    )
    return jax.shard_map(local, mesh=mesh, in_specs=in_specs, out_specs=out_specs, check_vma=False)
```

```python
import jax
import jax.numpy as jnp
from jax import lax
from jax.experimental import pallas as pl
from jax.experimental.pallas import tpu as pltpu
from jax.sharding import PartitionSpec as P

HEAD_DIM = 128
BLK = 128
EPS = 1e-05
THETA = 10000.0
NZ, NX, NC = 4, 4, 2
NY, NH = 4, 2
STATIC = 16
EXTRA = 4
MIB = 1024 * 1024

SMEM = pl.BlockSpec(memory_space=pltpu.SMEM)
VMEM = pl.BlockSpec(memory_space=pltpu.VMEM)
HBM = pl.BlockSpec(memory_space=pltpu.HBM)


def dp_perm(dz, dx, dc):
    pairs = []
    for z in range(NZ):
        for x in range(NX):
            for c in range(NC):
                src = (z * NX + x) * NC + c
                dst = (((z + dz) % NZ) * NX + (x + dx) % NX) * NC + (c + dc) % NC
                pairs.append((src, dst))
    return pairs


def send_dp(value, dz, dx, dc):
    return lax.ppermute(value, "dp", dp_perm(dz, dx, dc))


def send_tensor(value, dy, dh):
    pairs = []
    for y in range(NY):
        for h in range(NH):
            pairs.append((y * NH + h, ((y + dy) % NY) * NH + (h + dh) % NH))
    return lax.ppermute(value, "tensor", pairs)


def rope_tables(rows_len):
    half_dim = HEAD_DIM // 2
    positions = jnp.arange(rows_len, dtype=jnp.float32)
    freqs = jnp.exp(
        -jnp.log(THETA) * jnp.arange(half_dim, dtype=jnp.float32) * 2.0 / HEAD_DIM
    )
    angles = positions[:, None] * freqs[None, :]
    cosine = jnp.cos(angles)
    sine = jnp.sin(angles)
    return jnp.concatenate([cosine, cosine], 1), jnp.concatenate([-sine, sine], 1)


def block_tables(matrix, keep, owner, group, width, capacity):
    dp_index = lax.axis_index("dp")
    my_c = dp_index % NC
    my_x = (dp_index // NC) % NX
    my_z = dp_index // (NC * NX)
    rows_count = keep.shape[0]
    kept = lax.dynamic_slice_in_dim(keep, group * width, width, 1)
    owners = lax.dynamic_slice_in_dim(owner, group * width, width, 1)
    flat_kept = kept.reshape(-1)
    flat_owner = owners.reshape(-1)
    count = flat_kept.shape[0]
    order = jnp.arange(count, dtype=jnp.int32)
    same = (
        (flat_owner[:, None] == flat_owner[None, :])
        & (order[None, :] < order[:, None])
        & (flat_kept[None, :] == 1)
    )
    ranks = jnp.sum(same.astype(jnp.int32), axis=1)
    rel_c = (flat_owner + my_c) % NC
    rel_x = (flat_owner // NC + NX - my_x) % NX
    rel_z = (flat_owner // (NC * NX) + NZ - my_z) % NZ
    slots = NC * NX * NZ * capacity
    places = ((rel_c * NX + rel_x) * NZ + rel_z) * capacity + ranks
    places = jnp.where(flat_kept == 1, places, slots)
    line = NZ * capacity
    owner_z = flat_owner // (NC * NX)
    direct = (matrix * 3 + jnp.minimum(rel_x, 2)) * line + owner_z * capacity
    around = 6 * line + (owner_z // 2) * line + (matrix * 2 + owner_z % 2) * capacity
    stored = rel_c * slots + jnp.where(rel_x == 2, around, direct) + ranks
    hits = places[:, None] == jnp.arange(slots, dtype=jnp.int32)[None, :]
    code = jnp.sum(jnp.where(hits, order[:, None] + 1, 0), axis=0) - 1
    slot_row = jnp.where(code >= 0, code // width, 0)
    slot_col = jnp.where(code >= 0, code % width, width)
    grid_places = stored.reshape(rows_count, width)
    below = jnp.cumsum(kept, axis=0) - kept
    wanted = (below[:, :, None] == jnp.arange(rows_count, dtype=jnp.int32)[None, None, :]) & (
        kept[:, :, None] == 1
    )
    rows = jnp.arange(rows_count, dtype=jnp.int32)[:, None, None]
    list_row = jnp.sum(jnp.where(wanted, rows, 0), axis=0)
    list_place = 2 * slots + jnp.sum(
        jnp.where(wanted, grid_places[:, :, None] - 2 * slots, 0), axis=0
    )
    col_count = jnp.sum(kept, axis=0)
    return slot_row, slot_col, list_row, list_place, col_count


def attention_kernel(*refs):
    index_ref = refs[0]
    pieces = refs[1:9]
    wq_ref, wkv_ref, wo_ref, cos_ref, sin_ref, drow_ref, dcol_ref = refs[9:16]
    two_ref = refs[22]
    outs = [*refs[16:19], two_ref.at[0], *refs[19:22], two_ref.at[1]]
    wq_buf, wkv_buf, wo_buf, sem = refs[23:]
    rows_len, share = pieces[0].shape
    width = share * len(pieces)
    places = [pl.multiple_of(index_ref[i] * share, share) for i in range(len(pieces))]
    loads = []
    for i, at in enumerate(places):
        rows = pl.ds(at, share)
        loads.append(pltpu.make_async_copy(wq_ref.at[rows], wq_buf.at[i], sem.at[0, i]))
        loads.append(pltpu.make_async_copy(wkv_ref.at[rows], wkv_buf.at[i], sem.at[1, i]))
    loads.append(pltpu.make_async_copy(wo_ref, wo_buf, sem.at[0, len(pieces)]))
    for load in loads:
        load.start()
    q_acc = jnp.zeros((rows_len, wq_ref.shape[1]), jnp.float32)
    kv_acc = jnp.zeros((rows_len, wkv_ref.shape[1]), jnp.float32)
    squares = jnp.zeros((rows_len, 1), jnp.float32)
    for i, piece in enumerate(pieces):
        x = piece[...]
        loads[2 * i].wait()
        loads[2 * i + 1].wait()
        q_acc += jnp.dot(x, wq_buf[i], preferred_element_type=jnp.float32)
        kv_acc += jnp.dot(x, wkv_buf[i], preferred_element_type=jnp.float32)
        wide = x.astype(jnp.float32)
        squares += jnp.sum(wide * wide, axis=1, keepdims=True)
    scale = lax.rsqrt(squares / width + EPS)
    cosine = cos_ref[...]
    sine = sin_ref[...]

    def rotated(raw):
        normed = raw * scale
        return (normed * cosine + pltpu.roll(normed, HEAD_DIM // 2, 1) * sine).astype(jnp.bfloat16)

    key = rotated(kv_acc[:, :HEAD_DIM])
    value = (kv_acc[:, HEAD_DIM:] * scale).astype(jnp.bfloat16)
    q_pos = lax.broadcasted_iota(jnp.int32, (rows_len, rows_len), 0)
    k_pos = lax.broadcasted_iota(jnp.int32, (rows_len, rows_len), 1)
    allowed = (drow_ref[...] == dcol_ref[...]) & (k_pos <= q_pos)
    contexts = []
    for head in range(wq_ref.shape[1] // HEAD_DIM):
        query = rotated(q_acc[:, head * HEAD_DIM : (head + 1) * HEAD_DIM])
        scores = lax.dot_general(
            query, key, (((1,), (1,)), ((), ())), preferred_element_type=jnp.float32
        ) * (HEAD_DIM ** (-0.5))
        scores = jnp.where(allowed, scores, -1e30)
        highest = jnp.max(scores, axis=1, keepdims=True)
        weights = jnp.exp(scores - highest)
        probs = (weights / jnp.sum(weights, axis=1, keepdims=True)).astype(jnp.bfloat16)
        contexts.append(
            jnp.dot(probs, value, preferred_element_type=jnp.float32).astype(jnp.bfloat16)
        )
    context = jnp.concatenate(contexts, axis=1)
    loads[-1].wait()
    for out, at in zip(outs, places):
        out[...] = jnp.dot(
            context, wo_buf[:, pl.ds(at, share)], preferred_element_type=jnp.float32
        ).astype(jnp.bfloat16)


def forward_kernel(n_parts, index_ref, row_ref, place_ref, count_ref, *refs):
    pieces = refs[:8]
    cot_ref = refs[8]
    parts = refs[9 : 9 + n_parts]
    hidden_ref, dgate_ref, dup_ref, xt_ref, xb_ref, w_ref, sem = refs[9 + n_parts :]
    rows_len, share = pieces[0].shape
    per_piece = share // BLK
    model_width = share * len(pieces)
    width = dgate_ref.shape[0] - 1
    copies = []
    begin = 0
    for i, part in enumerate(parts):
        size = part.shape[0]
        copies.append(pltpu.make_async_copy(part, w_ref.at[pl.ds(begin, size)], sem.at[i]))
        begin += size
    for copy in copies:
        copy.start()
    w_ref[begin] = jnp.zeros((BLK, BLK), jnp.bfloat16)
    squares = jnp.zeros((rows_len, 1), jnp.float32)
    for i, piece in enumerate(pieces):
        x = piece[...]
        wide = x.astype(jnp.float32)
        squares += jnp.sum(wide * wide, axis=1, keepdims=True)
        for q in range(per_piece):
            block = x[:, q * BLK : (q + 1) * BLK]
            xb_ref[index_ref[i] * per_piece + q] = block
            xt_ref[index_ref[i] * per_piece + q] = block.T
    scale = lax.rsqrt(squares / model_width + EPS)
    dgate_ref[width] = jnp.zeros((rows_len, BLK), jnp.bfloat16)
    dup_ref[width] = jnp.zeros((rows_len, BLK), jnp.bfloat16)
    for copy in copies:
        copy.wait()

    def product(matrix, col, first, amount):
        x = [xb_ref[row_ref[matrix, col, first + k]] for k in range(amount)]
        w = [w_ref[place_ref[matrix, col, first + k]] for k in range(amount)]
        return jnp.dot(
            jnp.concatenate(x, 1), jnp.concatenate(w, 0), preferred_element_type=jnp.float32
        )

    def finish(col, gate, upper):
        gate = gate * scale
        upper = upper * scale
        at = pl.ds(pl.multiple_of(col * BLK, BLK), BLK)
        cot = cot_ref[:, at].astype(jnp.float32)
        sigma = 1.0 / (1.0 + jnp.exp(-gate))
        activ = gate * sigma
        hidden_ref[:, at] = (activ * upper).astype(jnp.bfloat16)
        scaled = cot * scale
        dgate_ref[col] = (scaled * upper * sigma * (1.0 + gate * (1.0 - sigma))).astype(jnp.bfloat16)
        dup_ref[col] = (scaled * activ).astype(jnp.bfloat16)

    def column(col, carry):
        most = jnp.maximum(count_ref[0, col], count_ref[1, col])

        @pl.when(most <= STATIC)
        def _():
            finish(col, product(0, col, 0, STATIC), product(1, col, 0, STATIC))

        @pl.when(most > STATIC)
        def _():
            more = (most - STATIC + EXTRA - 1) // EXTRA

            def step(n, sums):
                first = STATIC + n * EXTRA
                return tuple(sums[m] + product(m, col, first, EXTRA) for m in range(2))

            sums = tuple(product(m, col, 0, STATIC) for m in range(2))
            finish(col, *lax.fori_loop(0, more, step, sums))

        return carry

    lax.fori_loop(0, width, column, 0)


def term(xt_ref, grads_ref, row_ref, col_ref, slot):
    return jnp.dot(
        xt_ref[row_ref[slot]], grads_ref[col_ref[slot]], preferred_element_type=jnp.float32
    )


def far_kernel(first, unroll, row_ref, col_ref, xt_ref, grads_ref, out_ref):
    def step(n, carry):
        for k in range(unroll):
            slot = n * unroll + k
            out_ref[slot] = term(xt_ref, grads_ref, row_ref, col_ref, first + slot).astype(
                jnp.bfloat16
            )
        return carry

    lax.fori_loop(0, out_ref.shape[0] // unroll, step, 0)


def near_kernel(unroll, segments, row_ref, col_ref, xt_ref, grads_ref, add_ref, *outs):
    for out_ref, pieces in zip(outs, segments):
        at = 0
        for first, size in pieces:

            def step(n, carry, out_ref=out_ref, first=first, at=at):
                for k in range(unroll):
                    slot = n * unroll + k
                    value = term(xt_ref, grads_ref, row_ref, col_ref, first + slot)
                    value += add_ref[first + slot].astype(jnp.float32)
                    out_ref[at + slot] = value.astype(jnp.bfloat16)
                return carry

            lax.fori_loop(0, size // unroll, step, 0)
            at += size


def shape_of(shape, dtype=jnp.bfloat16):
    return jax.ShapeDtypeStruct(shape, dtype)


def params(mib):
    return pltpu.CompilerParams(vmem_limit_bytes=mib * MIB)


def wide_sum(*values):
    total = values[0].astype(jnp.float32)
    for value in values[1:]:
        total = total + value.astype(jnp.float32)
    return total


def tie(*values):
    return lax.optimization_barrier(values)


def gather_z(own):
    lines = [
        [(z * NX + x) * NC + c for z in range(NZ)] for x in range(NX) for c in range(NC)
    ]
    return lax.all_gather(own, "dp", axis=0, tiled=True, axis_index_groups=lines)


def send_x(value):
    return [send_dp(value, 0, 1, 0), send_dp(value, 0, 3, 0)]


def local(tokens, doc_ids, wq, wkv, wo, gate_blocks, up_blocks, keep_mask, owner_map, hidden_cot):
    group = lax.axis_index("tensor")
    my_y = group // NH
    my_h = group % NH
    capacity = gate_blocks.shape[2]
    rows_len, share = tokens.shape
    n_share = lax.axis_size("tensor")
    model_width = share * n_share
    width = hidden_cot.shape[1] // BLK
    bf16 = jnp.bfloat16

    places = jnp.stack(
        [((my_y + d) % NY) * NH + (my_h + h) % NH for h in range(NH) for d in (0, 3, 1, 2)]
    ).astype(jnp.int32)

    steps = (1, 3, 2)
    back = (3, 1, 2)
    own_blocks = jnp.concatenate([gate_blocks, up_blocks], axis=2).reshape(-1, BLK, BLK)
    tokens, own_blocks = tie(tokens, own_blocks)
    rows_z = gather_z(own_blocks)
    other = send_tensor(tokens, 0, 1)
    across = [send_tensor(tokens, d, 0) for d in steps]
    other, across = tie(other, across)
    pieces = [tokens, *across, other] + [send_tensor(other, d, 0) for d in steps]

    cosine, sine = rope_tables(rows_len)
    tables = [
        block_tables(m, keep_mask[m], owner_map[m], group, width, capacity) for m in range(2)
    ]
    list_row = jnp.stack([t[2] for t in tables])
    list_place = jnp.stack([t[3] for t in tables])
    col_count = jnp.stack([t[4] for t in tables])

    pieces[7], list_row, list_place, col_count, tables = tie(
        pieces[7], list_row, list_place, col_count, tables
    )

    partial = pl.pallas_call(
        attention_kernel,
        out_shape=[shape_of((rows_len, share))] * 6 + [shape_of((NH, rows_len, share))],
        in_specs=[SMEM] + [VMEM] * 8 + [HBM] * 3 + [VMEM] * 4,
        out_specs=[VMEM] * 7,
        scratch_shapes=[
            pltpu.VMEM((n_share, share, wq.shape[1]), bf16),
            pltpu.VMEM((n_share, share, 2 * wkv.shape[2]), bf16),
            pltpu.VMEM(wo.shape, bf16),
            pltpu.SemaphoreType.DMA((2, n_share + 1)),
        ],
        compiler_params=params(58),
        name="attention",
    )(
        places,
        *pieces,
        wq,
        wkv.reshape(model_width, -1),
        wo,
        cosine,
        sine,
        doc_ids.reshape(rows_len, 1),
        doc_ids.reshape(1, rows_len),
    )
    partial, rows_z = tie(list(partial), rows_z)
    rows_z = rows_z.reshape(NZ, 2, capacity, BLK, BLK)
    gate_z, up_z = [rows_z[:, m].reshape(NZ * capacity, BLK, BLK) for m in range(2)]
    half = NZ * capacity // 2
    got = [send_tensor(partial[4 + k], back[k], 0) for k in range(2)]
    two = send_tensor(partial[6], 2, 0)
    gate_x = send_x(gate_z)
    got, two, gate_x = tie(got, two, gate_x)

    crossed = wide_sum(partial[3], *got, two[1]).astype(bf16)
    from_other = send_tensor(crossed, 0, 1)
    direct = [send_tensor(partial[1 + k], back[k], 0) for k in range(2)]
    up_x = send_x(up_z)
    from_other, direct, up_x = tie(from_other, direct, up_x)

    mixed = wide_sum(tokens, partial[0], *direct, two[0], from_other).astype(bf16)
    left = jnp.concatenate([gate_x[0][:half], up_x[0][:half]], axis=0)
    right = jnp.concatenate([gate_x[1][half:], up_x[1][half:]], axis=0)
    mixed, left, right = tie(mixed, left, right)
    other = send_tensor(mixed, 0, 1)
    across = [send_tensor(mixed, d, 0) for d in steps[:2]]
    far_a = send_dp(left, 0, 1, 0)
    far_b = send_dp(right, 0, 3, 0)
    other, across, far_a, far_b = tie(other, across, far_a, far_b)

    two = send_tensor(jnp.stack([mixed, other]), 2, 0)
    mid = [mixed, *across, two[0], other, *[send_tensor(other, d, 0) for d in steps[:2]], two[1]]
    mine = [gate_z, gate_x[1], gate_x[0], up_z, up_x[1], up_x[0], far_a, far_b]
    parts = mine + [send_dp(jnp.concatenate(mine, axis=0), 0, 0, 1)]

    slots = NC * NX * NZ * capacity
    kernel = lambda *refs: forward_kernel(len(parts), *refs)
    hidden, d_gate, d_up, x_t = pl.pallas_call(
        kernel,
        out_shape=[
            shape_of((rows_len, width * BLK)),
            shape_of((width + 1, rows_len, BLK)),
            shape_of((width + 1, rows_len, BLK)),
            shape_of((model_width // BLK, BLK, rows_len)),
        ],
        in_specs=[SMEM] * 4 + [VMEM] * 9 + [HBM] * len(parts),
        out_specs=[VMEM] * 4,
        scratch_shapes=[
            pltpu.VMEM((model_width // BLK, rows_len, BLK), bf16),
            pltpu.VMEM((2 * slots + 1, BLK, BLK), bf16),
            pltpu.SemaphoreType.DMA((len(parts),)),
        ],
        compiler_params=params(40),
        name="forward",
    )(places, list_row, list_place, col_count, *mid, hidden_cot, *parts)

    side = slots // NC
    quarter = side // NX
    half = quarter // 2

    def far(m, grads):
        kernel = lambda *refs: far_kernel(side, 12, *refs)
        return pl.pallas_call(
            kernel,
            out_shape=shape_of((side, BLK, BLK)),
            in_specs=[SMEM] * 2 + [VMEM] * 2,
            out_specs=VMEM,
            compiler_params=params(16),
            name="far",
        )(tables[m][0], tables[m][1], x_t, grads)

    def near(m, grads, add):
        segments = (
            ((2 * quarter, half), (quarter + half, half)),
            ((2 * quarter + half, half), (3 * quarter, half)),
            ((quarter, half),),
            ((3 * quarter + half, half),),
            ((0, quarter),),
        )
        sizes = [sum(size for _, size in pieces) for pieces in segments]
        kernel = lambda *refs: near_kernel(12, segments, *refs)
        return pl.pallas_call(
            kernel,
            out_shape=[shape_of((size, BLK, BLK)) for size in sizes],
            in_specs=[SMEM] * 2 + [VMEM] * 3,
            out_specs=[VMEM] * len(sizes),
            compiler_params=params(16),
            name="near",
        )(tables[m][0], tables[m][1], x_t, grads, add)

    def reduce_rest(sums):
        to_right, to_left, s1a, s3b, s0 = sums
        left = send_dp(to_right, 0, 1, 0)
        right = send_dp(to_left, 0, 3, 0)
        from_left = send_dp(wide_sum(s1a, left[:half]).astype(bf16), 0, 1, 0)
        from_right = send_dp(wide_sum(s3b, right[:half]).astype(bf16), 0, 3, 0)
        sum_a = wide_sum(s0[:half], from_left, right[half:])
        sum_b = wide_sum(s0[half:], from_right, left[half:])
        by_z = [sum_a[:capacity], sum_a[capacity:], sum_b[:capacity], sum_b[capacity:]]
        total = wide_sum(by_z[0], *[send_dp(by_z[d].astype(bf16), d, 0, 0) for d in (1, 2, 3)])
        return total.reshape(1, 1, capacity, BLK, BLK)

    far_gate = far(0, d_gate)
    swap_gate = send_dp(far_gate, 0, 0, 1)
    far_up = far(1, d_up)
    swap_up = send_dp(far_up, 0, 0, 1)
    gate_grad = reduce_rest(near(0, d_gate, swap_gate))
    up_grad = reduce_rest(near(1, d_up, swap_up))
    return (mixed, hidden, gate_grad, up_grad)


def solution(mesh):
    in_specs = (
        P("dp", "tensor"),
        P("dp", None),
        P(None, "tensor"),
        P(None, None, "tensor"),
        P("tensor", None),
        P("dp", "tensor", None, None, None),
        P("dp", "tensor", None, None, None),
        P(),
        P(),
        P("dp", "tensor"),
    )
    out_specs = (
        P("dp", "tensor"),
        P("dp", "tensor"),
        P("dp", "tensor", None, None, None),
        P("dp", "tensor", None, None, None),
    )
    return jax.shard_map(local, mesh=mesh, in_specs=in_specs, out_specs=out_specs, check_vma=False)
```

```python
import jax
import jax.numpy as jnp
from jax import lax
from jax.experimental import pallas as pl
from jax.experimental.pallas import tpu as pltpu
from jax.sharding import PartitionSpec as P

HEAD_DIM = 128
BLK = 128
EPS = 1e-05
THETA = 10000.0
NZ, NX, NC = 4, 4, 2
NY, NH = 4, 2
STATIC = 8
EXTRA = 4
MIB = 1024 * 1024

SMEM = pl.BlockSpec(memory_space=pltpu.SMEM)
VMEM = pl.BlockSpec(memory_space=pltpu.VMEM)
HBM = pl.BlockSpec(memory_space=pltpu.HBM)


def dp_perm(dz, dx, dc):
    pairs = []
    for z in range(NZ):
        for x in range(NX):
            for c in range(NC):
                src = (z * NX + x) * NC + c
                dst = (((z + dz) % NZ) * NX + (x + dx) % NX) * NC + (c + dc) % NC
                pairs.append((src, dst))
    return pairs


def send_dp(value, dz, dx, dc):
    return lax.ppermute(value, "dp", dp_perm(dz, dx, dc))


def send_tensor(value, dy, dh):
    pairs = []
    for y in range(NY):
        for h in range(NH):
            pairs.append((y * NH + h, ((y + dy) % NY) * NH + (h + dh) % NH))
    return lax.ppermute(value, "tensor", pairs)


def rope_tables(rows_len):
    half_dim = HEAD_DIM // 2
    positions = jnp.arange(rows_len, dtype=jnp.float32)
    freqs = jnp.exp(
        -jnp.log(THETA) * jnp.arange(half_dim, dtype=jnp.float32) * 2.0 / HEAD_DIM
    )
    angles = positions[:, None] * freqs[None, :]
    cosine = jnp.cos(angles)
    sine = jnp.sin(angles)
    return jnp.concatenate([cosine, cosine], 1), jnp.concatenate([-sine, sine], 1)


def block_tables(matrix, keep, owner, group, width, capacity):
    dp_index = lax.axis_index("dp")
    my_c = dp_index % NC
    my_x = (dp_index // NC) % NX
    my_z = dp_index // (NC * NX)
    rows_count = keep.shape[0]
    kept = lax.dynamic_slice_in_dim(keep, group * width, width, 1)
    owners = lax.dynamic_slice_in_dim(owner, group * width, width, 1)
    flat_kept = kept.reshape(-1)
    flat_owner = owners.reshape(-1)
    count = flat_kept.shape[0]
    order = jnp.arange(count, dtype=jnp.int32)
    same = (
        (flat_owner[:, None] == flat_owner[None, :])
        & (order[None, :] < order[:, None])
        & (flat_kept[None, :] == 1)
    )
    ranks = jnp.sum(same.astype(jnp.int32), axis=1)
    rel_c = (flat_owner + my_c) % NC
    rel_x = (flat_owner // NC + NX - my_x) % NX
    rel_z = (flat_owner // (NC * NX) + NZ - my_z) % NZ
    slots = NC * NX * NZ * capacity
    places = ((rel_c * NX + rel_x) * NZ + rel_z) * capacity + ranks
    places = jnp.where(flat_kept == 1, places, slots)
    line = NZ * capacity
    beside = 2 + matrix * 2 + (rel_x == 1).astype(jnp.int32)
    direct = jnp.where(rel_x == 0, matrix, beside) * line + rel_z * capacity
    around = 6 * line + (rel_z // 2) * line + (matrix * 2 + rel_z % 2) * capacity
    stored = jnp.where(rel_x == 2, around, direct) + ranks
    hits = places[:, None] == jnp.arange(slots, dtype=jnp.int32)[None, :]
    code = jnp.sum(jnp.where(hits, order[:, None] + 1, 0), axis=0) - 1
    slot_row = jnp.where(code >= 0, code // width, 0)
    slot_col = jnp.where(code >= 0, code % width, width)
    core = rel_c.reshape(rows_count, width)
    sides = jnp.stack([kept * (core == c) for c in range(NC)])
    grid_places = stored.reshape(rows_count, width)
    below = jnp.cumsum(sides, axis=1) - sides
    numbers = jnp.arange(rows_count, dtype=jnp.int32)
    wanted = (below[..., None] == numbers) & (sides[..., None] == 1)
    list_row = jnp.sum(jnp.where(wanted, numbers[:, None, None], 0), axis=1)
    list_place = slots + jnp.sum(
        jnp.where(wanted, grid_places[:, :, None] - slots, 0), axis=1
    )
    col_count = jnp.sum(sides, axis=1)
    return slot_row, slot_col, list_row, list_place, col_count


def attention_kernel(*refs):
    index_ref = refs[0]
    pieces = refs[1:9]
    wq_ref, wkv_ref, wo_ref, cos_ref, sin_ref, drow_ref, dcol_ref = refs[9:16]
    two_ref = refs[22]
    outs = [*refs[16:19], two_ref.at[0], *refs[19:22], two_ref.at[1]]
    wq_buf, wkv_buf, wo_buf, sem = refs[23:]
    rows_len, share = pieces[0].shape
    width = share * len(pieces)
    places = [pl.multiple_of(index_ref[i] * share, share) for i in range(len(pieces))]
    loads = []
    for i, at in enumerate(places):
        rows = pl.ds(at, share)
        loads.append(pltpu.make_async_copy(wq_ref.at[rows], wq_buf.at[i], sem.at[0, i]))
        loads.append(pltpu.make_async_copy(wkv_ref.at[rows], wkv_buf.at[i], sem.at[1, i]))
    loads.append(pltpu.make_async_copy(wo_ref, wo_buf, sem.at[0, len(pieces)]))
    for load in loads:
        load.start()
    q_acc = jnp.zeros((rows_len, wq_ref.shape[1]), jnp.float32)
    kv_acc = jnp.zeros((rows_len, wkv_ref.shape[1]), jnp.float32)
    squares = jnp.zeros((rows_len, 1), jnp.float32)
    for i, piece in enumerate(pieces):
        x = piece[...]
        loads[2 * i].wait()
        loads[2 * i + 1].wait()
        q_acc += jnp.dot(x, wq_buf[i], preferred_element_type=jnp.float32)
        kv_acc += jnp.dot(x, wkv_buf[i], preferred_element_type=jnp.float32)
        wide = x.astype(jnp.float32)
        squares += jnp.sum(wide * wide, axis=1, keepdims=True)
    scale = lax.rsqrt(squares / width + EPS)
    cosine = cos_ref[...]
    sine = sin_ref[...]

    def rotated(raw):
        normed = raw * scale
        return (normed * cosine + pltpu.roll(normed, HEAD_DIM // 2, 1) * sine).astype(jnp.bfloat16)

    key = rotated(kv_acc[:, :HEAD_DIM])
    value = (kv_acc[:, HEAD_DIM:] * scale).astype(jnp.bfloat16)
    q_pos = lax.broadcasted_iota(jnp.int32, (rows_len, rows_len), 0)
    k_pos = lax.broadcasted_iota(jnp.int32, (rows_len, rows_len), 1)
    allowed = (drow_ref[...] == dcol_ref[...]) & (k_pos <= q_pos)
    contexts = []
    for head in range(wq_ref.shape[1] // HEAD_DIM):
        query = rotated(q_acc[:, head * HEAD_DIM : (head + 1) * HEAD_DIM])
        scores = lax.dot_general(
            query, key, (((1,), (1,)), ((), ())), preferred_element_type=jnp.float32
        ) * (HEAD_DIM ** (-0.5))
        scores = jnp.where(allowed, scores, -1e30)
        highest = jnp.max(scores, axis=1, keepdims=True)
        weights = jnp.exp(scores - highest)
        probs = (weights / jnp.sum(weights, axis=1, keepdims=True)).astype(jnp.bfloat16)
        contexts.append(
            jnp.dot(probs, value, preferred_element_type=jnp.float32).astype(jnp.bfloat16)
        )
    context = jnp.concatenate(contexts, axis=1)
    loads[-1].wait()
    for out, at in zip(outs, places):
        out[...] = jnp.dot(
            context, wo_buf[:, pl.ds(at, share)], preferred_element_type=jnp.float32
        ).astype(jnp.bfloat16)


def start_loads(parts, w_ref, sem):
    copies = []
    begin = 0
    for i, part in enumerate(parts):
        size = part.shape[0]
        copies.append(pltpu.make_async_copy(part, w_ref.at[pl.ds(begin, size)], sem.at[i]))
        begin += size
    for copy in copies:
        copy.start()
    w_ref[w_ref.shape[0] - 1] = jnp.zeros((BLK, BLK), jnp.bfloat16)
    return copies


def each_column(width, row_ref, place_ref, count_ref, xb_ref, w_ref, finish):
    def product(matrix, col, first, amount):
        x = [xb_ref[row_ref[matrix, col, first + k]] for k in range(amount)]
        w = [w_ref[place_ref[matrix, col, first + k]] for k in range(amount)]
        return jnp.dot(
            jnp.concatenate(x, 1), jnp.concatenate(w, 0), preferred_element_type=jnp.float32
        )

    def column(col, carry):
        most = jnp.maximum(count_ref[0, col], count_ref[1, col])

        @pl.when(most <= STATIC)
        def _():
            finish(col, product(0, col, 0, STATIC), product(1, col, 0, STATIC))

        @pl.when(most > STATIC)
        def _():
            more = (most - STATIC + EXTRA - 1) // EXTRA

            def step(n, sums):
                first = STATIC + n * EXTRA
                return tuple(sums[m] + product(m, col, first, EXTRA) for m in range(2))

            sums = tuple(product(m, col, 0, STATIC) for m in range(2))
            finish(col, *lax.fori_loop(0, more, step, sums))

        return carry

    lax.fori_loop(0, width, column, 0)


def first_kernel(index_ref, row_ref, place_ref, count_ref, *refs):
    pieces = refs[:8]
    parts = refs[8:-6]
    xb_ref, xt_ref, scale_ref, sums_ref, w_ref, sem = refs[-6:]
    rows_len, share = pieces[0].shape
    per_piece = share // BLK
    copies = start_loads(parts, w_ref, sem)
    squares = jnp.zeros((rows_len, 1), jnp.float32)
    for i, piece in enumerate(pieces):
        x = piece[...]
        wide = x.astype(jnp.float32)
        squares += jnp.sum(wide * wide, axis=1, keepdims=True)
        for q in range(per_piece):
            block = x[:, q * BLK : (q + 1) * BLK]
            xb_ref[index_ref[i] * per_piece + q] = block
            xt_ref[index_ref[i] * per_piece + q] = block.T
    scale = lax.rsqrt(squares / (share * len(pieces)) + EPS)
    scale_ref[...] = jnp.broadcast_to(scale, scale_ref.shape)
    for copy in copies:
        copy.wait()

    def finish(col, gate, upper):
        sums_ref[0, col] = gate
        sums_ref[1, col] = upper

    each_column(sums_ref.shape[1], row_ref, place_ref, count_ref, xb_ref, w_ref, finish)


def second_kernel(row_ref, place_ref, count_ref, xb_ref, scale_ref, sums_ref, cot_ref, *refs):
    parts = refs[:-5]
    hidden_ref, dgate_ref, dup_ref, w_ref, sem = refs[-5:]
    width = sums_ref.shape[1]
    copies = start_loads(parts, w_ref, sem)
    dgate_ref[width] = jnp.zeros_like(dgate_ref[width])
    dup_ref[width] = jnp.zeros_like(dup_ref[width])
    scale = scale_ref[...]
    for copy in copies:
        copy.wait()

    def finish(col, gate, upper):
        gate = (gate + sums_ref[0, col]) * scale
        upper = (upper + sums_ref[1, col]) * scale
        at = pl.ds(pl.multiple_of(col * BLK, BLK), BLK)
        cot = cot_ref[:, at].astype(jnp.float32)
        sigma = 1.0 / (1.0 + jnp.exp(-gate))
        activ = gate * sigma
        hidden_ref[:, at] = (activ * upper).astype(jnp.bfloat16)
        scaled = cot * scale
        dgate_ref[col] = (scaled * upper * sigma * (1.0 + gate * (1.0 - sigma))).astype(jnp.bfloat16)
        dup_ref[col] = (scaled * activ).astype(jnp.bfloat16)

    each_column(width, row_ref, place_ref, count_ref, xb_ref, w_ref, finish)


def term(xt_ref, grads_ref, row_ref, col_ref, slot):
    return jnp.dot(
        xt_ref[row_ref[slot]], grads_ref[col_ref[slot]], preferred_element_type=jnp.float32
    )


def far_kernel(first, unroll, row_ref, col_ref, xt_ref, grads_ref, out_ref):
    def step(n, carry):
        for k in range(unroll):
            slot = n * unroll + k
            out_ref[slot] = term(xt_ref, grads_ref, row_ref, col_ref, first + slot).astype(
                jnp.bfloat16
            )
        return carry

    lax.fori_loop(0, out_ref.shape[0] // unroll, step, 0)


def near_kernel(unroll, segments, row_ref, col_ref, xt_ref, grads_ref, add_ref, *outs):
    for out_ref, pieces in zip(outs, segments):
        at = 0
        for first, size in pieces:

            def step(n, carry, out_ref=out_ref, first=first, at=at):
                for k in range(unroll):
                    slot = n * unroll + k
                    value = term(xt_ref, grads_ref, row_ref, col_ref, first + slot)
                    value += add_ref[first + slot].astype(jnp.float32)
                    out_ref[at + slot] = value.astype(jnp.bfloat16)
                return carry

            lax.fori_loop(0, size // unroll, step, 0)
            at += size


def shape_of(shape, dtype=jnp.bfloat16):
    return jax.ShapeDtypeStruct(shape, dtype)


def params(mib):
    return pltpu.CompilerParams(vmem_limit_bytes=mib * MIB)


def wide_sum(*values):
    total = values[0].astype(jnp.float32)
    for value in values[1:]:
        total = total + value.astype(jnp.float32)
    return total


def tie(*values):
    return lax.optimization_barrier(values)


def send_x(value):
    return [send_dp(value, 0, 1, 0), send_dp(value, 0, 3, 0)]


def local(tokens, doc_ids, wq, wkv, wo, gate_blocks, up_blocks, keep_mask, owner_map, hidden_cot):
    group = lax.axis_index("tensor")
    my_y = group // NH
    my_h = group % NH
    capacity = gate_blocks.shape[2]
    rows_len, share = tokens.shape
    n_share = lax.axis_size("tensor")
    model_width = share * n_share
    width = hidden_cot.shape[1] // BLK
    bf16 = jnp.bfloat16

    places = jnp.stack(
        [((my_y + d) % NY) * NH + (my_h + h) % NH for h in range(NH) for d in (0, 3, 1, 2)]
    ).astype(jnp.int32)

    steps = (1, 3, 2)
    back = (3, 1, 2)
    own_blocks = jnp.concatenate([gate_blocks, up_blocks], axis=2).reshape(-1, BLK, BLK)
    other = send_tensor(tokens, 0, 1)
    across = [send_tensor(tokens, d, 0) for d in steps]
    other, across, own_blocks = tie(other, across, own_blocks)
    pieces = [tokens, *across, other] + [send_tensor(other, d, 0) for d in steps]
    z_two = send_dp(own_blocks, 2, 0, 0)

    cosine, sine = rope_tables(rows_len)
    tables = [
        block_tables(m, keep_mask[m], owner_map[m], group, width, capacity) for m in range(2)
    ]
    list_row = jnp.stack([t[2] for t in tables], axis=1)
    list_place = jnp.stack([t[3] for t in tables], axis=1)
    col_count = jnp.stack([t[4] for t in tables], axis=1)

    pieces[7], list_row, list_place, col_count, tables = tie(
        pieces[7], list_row, list_place, col_count, tables
    )

    partial = pl.pallas_call(
        attention_kernel,
        out_shape=[shape_of((rows_len, share))] * 6 + [shape_of((NH, rows_len, share))],
        in_specs=[SMEM] + [VMEM] * 8 + [HBM] * 3 + [VMEM] * 4,
        out_specs=[VMEM] * 7,
        scratch_shapes=[
            pltpu.VMEM((n_share, share, wq.shape[1]), bf16),
            pltpu.VMEM((n_share, share, 2 * wkv.shape[2]), bf16),
            pltpu.VMEM(wo.shape, bf16),
            pltpu.SemaphoreType.DMA((2, n_share + 1)),
        ],
        compiler_params=params(58),
        name="attention",
    )(
        places,
        *pieces,
        wq,
        wkv.reshape(model_width, -1),
        wo,
        cosine,
        sine,
        doc_ids.reshape(rows_len, 1),
        doc_ids.reshape(1, rows_len),
    )
    partial, z_two, own_blocks = tie(list(partial), z_two, own_blocks)
    got = [send_tensor(partial[4 + k], back[k], 0) for k in range(2)]
    two = send_tensor(partial[6], 2, 0)
    z_one = send_dp(own_blocks, 3, 0, 0)
    z_three = send_dp(own_blocks, 1, 0, 0)
    got, two, z_one, z_three = tie(got, two, z_one, z_three)

    rows_z = (own_blocks, z_one, z_two, z_three)
    gate_z, up_z = [
        jnp.concatenate([row[m * capacity : (m + 1) * capacity] for row in rows_z], axis=0)
        for m in range(2)
    ]
    half = NZ * capacity // 2
    crossed = wide_sum(partial[3], *got, two[1]).astype(bf16)
    from_other = send_tensor(crossed, 0, 1)
    direct = [send_tensor(partial[1 + k], back[k], 0) for k in range(2)]
    gate_x = send_x(gate_z)
    from_other, direct, gate_x, up_z = tie(from_other, direct, gate_x, up_z)

    mixed = wide_sum(tokens, partial[0], *direct, two[0], from_other).astype(bf16)
    other = send_tensor(mixed, 0, 1)
    across = [send_tensor(mixed, d, 0) for d in steps[:2]]
    up_x = send_x(up_z)
    other, across, up_x = tie(other, across, up_x)

    two = send_tensor(jnp.stack([mixed, other]), 2, 0)
    mid = [mixed, *across, two[0], other, *[send_tensor(other, d, 0) for d in steps[:2]], two[1]]
    far_a = send_dp(jnp.concatenate([gate_x[0][:half], up_x[0][:half]], axis=0), 0, 1, 0)
    far_b = send_dp(jnp.concatenate([gate_x[1][half:], up_x[1][half:]], axis=0), 0, 3, 0)
    mid[5], mid[6], two, far_a, far_b = tie(mid[5], mid[6], two, far_a, far_b)
    mid[3], mid[7] = two[0], two[1]
    mine = [gate_z, up_z, *gate_x, *up_x, far_a, far_b]
    both = [jnp.concatenate(pair, axis=0) for pair in ((gate_z, up_z), gate_x, up_x)]
    swapped = [send_dp(part, 0, 0, 1) for part in (*both, far_a, far_b)]

    slots = NC * NX * NZ * capacity
    blocks = model_width // BLK
    scratch = [
        pltpu.VMEM((slots + 1, BLK, BLK), bf16),
        pltpu.SemaphoreType.DMA((len(mine),)),
    ]
    x_b, x_t, scale, sums = pl.pallas_call(
        first_kernel,
        out_shape=[
            shape_of((blocks, rows_len, BLK)),
            shape_of((blocks, BLK, rows_len)),
            shape_of((rows_len, BLK), jnp.float32),
            shape_of((2, width, rows_len, BLK), jnp.float32),
        ],
        in_specs=[SMEM] * 4 + [VMEM] * 8 + [HBM] * len(mine),
        out_specs=[VMEM] * 4,
        scratch_shapes=scratch,
        compiler_params=params(40),
        name="first",
    )(places, list_row[0], list_place[0], col_count[0], *mid, *mine)
    hidden, d_gate, d_up = pl.pallas_call(
        second_kernel,
        out_shape=[
            shape_of((rows_len, width * BLK)),
            shape_of((width + 1, rows_len, BLK)),
            shape_of((width + 1, rows_len, BLK)),
        ],
        in_specs=[SMEM] * 3 + [VMEM] * 4 + [HBM] * len(swapped),
        out_specs=[VMEM] * 3,
        scratch_shapes=scratch,
        compiler_params=params(40),
        name="second",
    )(list_row[1], list_place[1], col_count[1], x_b, scale, sums, hidden_cot, *swapped)

    side = slots // NC
    quarter = side // NX
    half = quarter // 2

    def far(m, grads):
        kernel = lambda *refs: far_kernel(side, 12, *refs)
        return pl.pallas_call(
            kernel,
            out_shape=shape_of((side, BLK, BLK)),
            in_specs=[SMEM] * 2 + [VMEM] * 2,
            out_specs=VMEM,
            compiler_params=params(16),
            name="far",
        )(tables[m][0], tables[m][1], x_t, grads)

    def near(m, grads, add):
        segments = (
            ((2 * quarter, half), (quarter + half, half)),
            ((2 * quarter + half, half), (3 * quarter, half)),
            ((quarter, half),),
            ((3 * quarter + half, half),),
            ((0, quarter),),
        )
        sizes = [sum(size for _, size in pieces) for pieces in segments]
        kernel = lambda *refs: near_kernel(12, segments, *refs)
        return pl.pallas_call(
            kernel,
            out_shape=[shape_of((size, BLK, BLK)) for size in sizes],
            in_specs=[SMEM] * 2 + [VMEM] * 3,
            out_specs=[VMEM] * len(sizes),
            compiler_params=params(16),
            name="near",
        )(tables[m][0], tables[m][1], x_t, grads, add)

    def send_first(sums):
        return send_dp(sums[0], 0, 1, 0), send_dp(sums[1], 0, 3, 0)

    def send_second(sums, left, right):
        from_left = send_dp(wide_sum(sums[2], left[:half]).astype(bf16), 0, 1, 0)
        from_right = send_dp(wide_sum(sums[3], right[:half]).astype(bf16), 0, 3, 0)
        return left, right, from_left, from_right

    def send_z(sums, left, right, from_left, from_right):
        sum_a = wide_sum(sums[4][:half], from_left, right[half:])
        sum_b = wide_sum(sums[4][half:], from_right, left[half:])
        by_z = [sum_a[:capacity], sum_a[capacity:], sum_b[:capacity], sum_b[capacity:]]
        return [by_z[0]] + [send_dp(by_z[d].astype(bf16), d, 0, 0) for d in (1, 2, 3)]

    def finish(terms):
        return wide_sum(*terms).reshape(1, 1, capacity, BLK, BLK)

    far_gate = far(0, d_gate)
    swap_gate = send_dp(far_gate, 0, 0, 1)
    far_up = far(1, d_up)
    swap_up = send_dp(far_up, 0, 0, 1)
    gate_sums = near(0, d_gate, swap_gate)
    up_sums = list(near(1, d_up, swap_up))
    got = send_second(gate_sums, *send_first(gate_sums))
    got, up_sums[0], up_sums[1] = tie(got, up_sums[0], up_sums[1])
    gate_terms = send_z(gate_sums, *got)
    first, gate_terms = tie(send_first(up_sums), gate_terms)
    gate_grad = finish(gate_terms)
    up_grad = finish(send_z(up_sums, *send_second(up_sums, *first)))
    return (mixed, hidden, gate_grad, up_grad)


def solution(mesh):
    in_specs = (
        P("dp", "tensor"),
        P("dp", None),
        P(None, "tensor"),
        P(None, None, "tensor"),
        P("tensor", None),
        P("dp", "tensor", None, None, None),
        P("dp", "tensor", None, None, None),
        P(),
        P(),
        P("dp", "tensor"),
    )
    out_specs = (
        P("dp", "tensor"),
        P("dp", "tensor"),
        P("dp", "tensor", None, None, None),
        P("dp", "tensor", None, None, None),
    )
    return jax.shard_map(local, mesh=mesh, in_specs=in_specs, out_specs=out_specs, check_vma=False)
```

```python
import jax
import jax.numpy as jnp
from jax import lax
from jax.experimental import pallas as pl
from jax.experimental.pallas import tpu as pltpu
from jax.sharding import PartitionSpec as P

HEAD_DIM = 128
BLK = 128
EPS = 1e-05
THETA = 10000.0
NZ, NX, NC = 4, 4, 2
NY, NH = 4, 2
STATIC = 8
EXTRA = 4
MIB = 1024 * 1024

SMEM = pl.BlockSpec(memory_space=pltpu.SMEM)
VMEM = pl.BlockSpec(memory_space=pltpu.VMEM)
HBM = pl.BlockSpec(memory_space=pltpu.HBM)


def dp_perm(dz, dx, dc):
    pairs = []
    for z in range(NZ):
        for x in range(NX):
            for c in range(NC):
                src = (z * NX + x) * NC + c
                dst = (((z + dz) % NZ) * NX + (x + dx) % NX) * NC + (c + dc) % NC
                pairs.append((src, dst))
    return pairs


def send_dp(value, dz, dx, dc):
    return lax.ppermute(value, "dp", dp_perm(dz, dx, dc))


def send_tensor(value, dy, dh):
    pairs = []
    for y in range(NY):
        for h in range(NH):
            pairs.append((y * NH + h, ((y + dy) % NY) * NH + (h + dh) % NH))
    return lax.ppermute(value, "tensor", pairs)


def rope_tables(rows_len):
    half_dim = HEAD_DIM // 2
    positions = jnp.arange(rows_len, dtype=jnp.float32)
    freqs = jnp.exp(
        -jnp.log(THETA) * jnp.arange(half_dim, dtype=jnp.float32) * 2.0 / HEAD_DIM
    )
    angles = positions[:, None] * freqs[None, :]
    cosine = jnp.cos(angles)
    sine = jnp.sin(angles)
    return jnp.concatenate([cosine, cosine], 1), jnp.concatenate([-sine, sine], 1)


def block_tables(matrix, keep, owner, group, width, capacity):
    dp_index = lax.axis_index("dp")
    my_c = dp_index % NC
    my_x = (dp_index // NC) % NX
    my_z = dp_index // (NC * NX)
    rows_count = keep.shape[0]
    kept = lax.dynamic_slice_in_dim(keep, group * width, width, 1)
    owners = lax.dynamic_slice_in_dim(owner, group * width, width, 1)
    flat_kept = kept.reshape(-1)
    flat_owner = owners.reshape(-1)
    count = flat_kept.shape[0]
    order = jnp.arange(count, dtype=jnp.int32)
    same = (
        (flat_owner[:, None] == flat_owner[None, :])
        & (order[None, :] < order[:, None])
        & (flat_kept[None, :] == 1)
    )
    ranks = jnp.sum(same.astype(jnp.int32), axis=1)
    rel_c = (flat_owner + my_c) % NC
    rel_x = (flat_owner // NC + NX - my_x) % NX
    rel_z = (flat_owner // (NC * NX) + NZ - my_z) % NZ
    slots = NC * NX * NZ * capacity
    places = ((rel_c * NX + rel_x) * NZ + rel_z) * capacity + ranks
    places = jnp.where(flat_kept == 1, places, slots)
    line = NZ * capacity
    beside = 2 + matrix * 2 + (rel_x == 1).astype(jnp.int32)
    direct = jnp.where(rel_x == 0, matrix, beside) * line + rel_z * capacity
    around = 6 * line + (rel_z // 2) * line + (matrix * 2 + rel_z % 2) * capacity
    stored = jnp.where(rel_x == 2, around, direct) + ranks
    hits = places[:, None] == jnp.arange(slots, dtype=jnp.int32)[None, :]
    code = jnp.sum(jnp.where(hits, order[:, None] + 1, 0), axis=0) - 1
    slot_row = jnp.where(code >= 0, code // width, 0)
    slot_col = jnp.where(code >= 0, code % width, width)
    core = rel_c.reshape(rows_count, width)
    sides = jnp.stack([kept * (core == c) for c in range(NC)])
    grid_places = stored.reshape(rows_count, width)
    below = jnp.cumsum(sides, axis=1) - sides
    numbers = jnp.arange(rows_count, dtype=jnp.int32)
    wanted = (below[..., None] == numbers) & (sides[..., None] == 1)
    list_row = jnp.sum(jnp.where(wanted, numbers[:, None, None], 0), axis=1)
    list_place = slots + jnp.sum(
        jnp.where(wanted, grid_places[:, :, None] - slots, 0), axis=1
    )
    col_count = jnp.sum(sides, axis=1)
    return slot_row, slot_col, list_row, list_place, col_count


def attention_kernel(*refs):
    index_ref = refs[0]
    pieces = refs[1:9]
    wq_ref, wkv_ref, wo_ref, cos_ref, sin_ref, drow_ref, dcol_ref = refs[9:16]
    two_ref = refs[22]
    outs = [*refs[16:19], two_ref.at[0], *refs[19:22], two_ref.at[1]]
    wq_buf, wkv_buf, wo_buf, sem = refs[23:]
    rows_len, share = pieces[0].shape
    width = share * len(pieces)
    places = [pl.multiple_of(index_ref[i] * share, share) for i in range(len(pieces))]
    loads = []
    for i, at in enumerate(places):
        rows = pl.ds(at, share)
        loads.append(pltpu.make_async_copy(wq_ref.at[rows], wq_buf.at[i], sem.at[0, i]))
        loads.append(pltpu.make_async_copy(wkv_ref.at[rows], wkv_buf.at[i], sem.at[1, i]))
    loads.append(pltpu.make_async_copy(wo_ref, wo_buf, sem.at[0, len(pieces)]))
    for load in loads:
        load.start()
    q_acc = jnp.zeros((rows_len, wq_ref.shape[1]), jnp.float32)
    kv_acc = jnp.zeros((rows_len, wkv_ref.shape[1]), jnp.float32)
    squares = jnp.zeros((rows_len, 1), jnp.float32)
    for i, piece in enumerate(pieces):
        x = piece[...]
        loads[2 * i].wait()
        loads[2 * i + 1].wait()
        q_acc += jnp.dot(x, wq_buf[i], preferred_element_type=jnp.float32)
        kv_acc += jnp.dot(x, wkv_buf[i], preferred_element_type=jnp.float32)
        wide = x.astype(jnp.float32)
        squares += jnp.sum(wide * wide, axis=1, keepdims=True)
    scale = lax.rsqrt(squares / width + EPS)
    cosine = cos_ref[...]
    sine = sin_ref[...]

    def rotated(raw):
        normed = raw * scale
        return (normed * cosine + pltpu.roll(normed, HEAD_DIM // 2, 1) * sine).astype(jnp.bfloat16)

    key = rotated(kv_acc[:, :HEAD_DIM])
    value = (kv_acc[:, HEAD_DIM:] * scale).astype(jnp.bfloat16)
    q_pos = lax.broadcasted_iota(jnp.int32, (rows_len, rows_len), 0)
    k_pos = lax.broadcasted_iota(jnp.int32, (rows_len, rows_len), 1)
    allowed = (drow_ref[...] == dcol_ref[...]) & (k_pos <= q_pos)
    contexts = []
    for head in range(wq_ref.shape[1] // HEAD_DIM):
        query = rotated(q_acc[:, head * HEAD_DIM : (head + 1) * HEAD_DIM])
        scores = lax.dot_general(
            query, key, (((1,), (1,)), ((), ())), preferred_element_type=jnp.float32
        ) * (HEAD_DIM ** (-0.5))
        scores = jnp.where(allowed, scores, -1e30)
        highest = jnp.max(scores, axis=1, keepdims=True)
        weights = jnp.exp(scores - highest)
        probs = (weights / jnp.sum(weights, axis=1, keepdims=True)).astype(jnp.bfloat16)
        contexts.append(
            jnp.dot(probs, value, preferred_element_type=jnp.float32).astype(jnp.bfloat16)
        )
    context = jnp.concatenate(contexts, axis=1)
    loads[-1].wait()
    for out, at in zip(outs, places):
        out[...] = jnp.dot(
            context, wo_buf[:, pl.ds(at, share)], preferred_element_type=jnp.float32
        ).astype(jnp.bfloat16)


def start_loads(parts, w_ref, sem):
    copies = []
    begin = 0
    for i, part in enumerate(parts):
        size = part.shape[0]
        copies.append(pltpu.make_async_copy(part, w_ref.at[pl.ds(begin, size)], sem.at[i]))
        begin += size
    for copy in copies:
        copy.start()
    w_ref[w_ref.shape[0] - 1] = jnp.zeros((BLK, BLK), jnp.bfloat16)
    return copies


def each_column(width, row_ref, place_ref, count_ref, xb_ref, w_ref, finish):
    def product(matrix, col, first, amount):
        x = [xb_ref[row_ref[matrix, col, first + k]] for k in range(amount)]
        w = [w_ref[place_ref[matrix, col, first + k]] for k in range(amount)]
        return jnp.dot(
            jnp.concatenate(x, 1), jnp.concatenate(w, 0), preferred_element_type=jnp.float32
        )

    def column(col, carry):
        most = jnp.maximum(count_ref[0, col], count_ref[1, col])

        @pl.when(most <= STATIC)
        def _():
            finish(col, product(0, col, 0, STATIC), product(1, col, 0, STATIC))

        @pl.when(most > STATIC)
        def _():
            more = (most - STATIC + EXTRA - 1) // EXTRA

            def step(n, sums):
                first = STATIC + n * EXTRA
                return tuple(sums[m] + product(m, col, first, EXTRA) for m in range(2))

            sums = tuple(product(m, col, 0, STATIC) for m in range(2))
            finish(col, *lax.fori_loop(0, more, step, sums))

        return carry

    lax.fori_loop(0, width, column, 0)


def first_kernel(index_ref, row_ref, place_ref, count_ref, *refs):
    pieces = refs[:8]
    parts = refs[8:-6]
    xb_ref, xt_ref, scale_ref, sums_ref, w_ref, sem = refs[-6:]
    rows_len, share = pieces[0].shape
    per_piece = share // BLK
    copies = start_loads(parts, w_ref, sem)
    squares = jnp.zeros((rows_len, 1), jnp.float32)
    for i, piece in enumerate(pieces):
        x = piece[...]
        wide = x.astype(jnp.float32)
        squares += jnp.sum(wide * wide, axis=1, keepdims=True)
        for q in range(per_piece):
            block = x[:, q * BLK : (q + 1) * BLK]
            xb_ref[index_ref[i] * per_piece + q] = block
            xt_ref[index_ref[i] * per_piece + q] = block.T
    scale = lax.rsqrt(squares / (share * len(pieces)) + EPS)
    scale_ref[...] = jnp.broadcast_to(scale, scale_ref.shape)
    for copy in copies:
        copy.wait()

    def finish(col, gate, upper):
        sums_ref[0, col] = gate
        sums_ref[1, col] = upper

    each_column(sums_ref.shape[1], row_ref, place_ref, count_ref, xb_ref, w_ref, finish)


def second_kernel(row_ref, place_ref, count_ref, xb_ref, scale_ref, sums_ref, cot_ref, *refs):
    parts = refs[:-5]
    hidden_ref, dgate_ref, dup_ref, w_ref, sem = refs[-5:]
    width = sums_ref.shape[1]
    copies = start_loads(parts, w_ref, sem)
    dgate_ref[width] = jnp.zeros_like(dgate_ref[width])
    dup_ref[width] = jnp.zeros_like(dup_ref[width])
    scale = scale_ref[...]
    for copy in copies:
        copy.wait()

    def finish(col, gate, upper):
        gate = (gate + sums_ref[0, col]) * scale
        upper = (upper + sums_ref[1, col]) * scale
        at = pl.ds(pl.multiple_of(col * BLK, BLK), BLK)
        cot = cot_ref[:, at].astype(jnp.float32)
        sigma = 1.0 / (1.0 + jnp.exp(-gate))
        activ = gate * sigma
        hidden_ref[:, at] = (activ * upper).astype(jnp.bfloat16)
        scaled = cot * scale
        dgate_ref[col] = (scaled * upper * sigma * (1.0 + gate * (1.0 - sigma))).astype(jnp.bfloat16)
        dup_ref[col] = (scaled * activ).astype(jnp.bfloat16)

    each_column(width, row_ref, place_ref, count_ref, xb_ref, w_ref, finish)


def term(xt_ref, grads_ref, row_ref, col_ref, slot):
    return jnp.dot(
        xt_ref[row_ref[slot]], grads_ref[col_ref[slot]], preferred_element_type=jnp.float32
    )


def far_kernel(first, unroll, row_ref, col_ref, xt_ref, grads_ref, out_ref):
    def step(n, carry):
        for k in range(unroll):
            slot = n * unroll + k
            out_ref[slot] = term(xt_ref, grads_ref, row_ref, col_ref, first + slot).astype(
                jnp.bfloat16
            )
        return carry

    lax.fori_loop(0, out_ref.shape[0] // unroll, step, 0)


def near_kernel(unroll, segments, row_ref, col_ref, xt_ref, grads_ref, add_ref, *outs):
    for out_ref, pieces in zip(outs, segments):
        at = 0
        for first, size in pieces:

            def step(n, carry, out_ref=out_ref, first=first, at=at):
                for k in range(unroll):
                    slot = n * unroll + k
                    value = term(xt_ref, grads_ref, row_ref, col_ref, first + slot)
                    value += add_ref[first + slot].astype(jnp.float32)
                    out_ref[at + slot] = value.astype(jnp.bfloat16)
                return carry

            lax.fori_loop(0, size // unroll, step, 0)
            at += size


def shape_of(shape, dtype=jnp.bfloat16):
    return jax.ShapeDtypeStruct(shape, dtype)


def params(mib):
    return pltpu.CompilerParams(vmem_limit_bytes=mib * MIB)


def wide_sum(*values):
    total = values[0].astype(jnp.float32)
    for value in values[1:]:
        total = total + value.astype(jnp.float32)
    return total


def tie(*values):
    return lax.optimization_barrier(values)


def send_x(value):
    return [send_dp(value, 0, 1, 0), send_dp(value, 0, 3, 0)]


def local(tokens, doc_ids, wq, wkv, wo, gate_blocks, up_blocks, keep_mask, owner_map, hidden_cot):
    group = lax.axis_index("tensor")
    my_y = group // NH
    my_h = group % NH
    capacity = gate_blocks.shape[2]
    rows_len, share = tokens.shape
    n_share = lax.axis_size("tensor")
    model_width = share * n_share
    width = hidden_cot.shape[1] // BLK
    bf16 = jnp.bfloat16

    places = jnp.stack(
        [((my_y + d) % NY) * NH + (my_h + h) % NH for h in range(NH) for d in (0, 3, 1, 2)]
    ).astype(jnp.int32)

    steps = (1, 3, 2)
    back = (3, 1, 2)
    own_blocks = jnp.concatenate([gate_blocks, up_blocks], axis=2).reshape(-1, BLK, BLK)
    other = send_tensor(tokens, 0, 1)
    across = [send_tensor(tokens, d, 0) for d in steps]
    other, across, own_blocks = tie(other, across, own_blocks)
    pieces = [tokens, *across, other] + [send_tensor(other, d, 0) for d in steps]
    z_two = send_dp(own_blocks, 2, 0, 0)

    cosine, sine = rope_tables(rows_len)
    tables = [
        block_tables(m, keep_mask[m], owner_map[m], group, width, capacity) for m in range(2)
    ]
    list_row = jnp.stack([t[2] for t in tables], axis=1)
    list_place = jnp.stack([t[3] for t in tables], axis=1)
    col_count = jnp.stack([t[4] for t in tables], axis=1)

    pieces[7], list_row, list_place, col_count, tables = tie(
        pieces[7], list_row, list_place, col_count, tables
    )

    partial = pl.pallas_call(
        attention_kernel,
        out_shape=[shape_of((rows_len, share))] * 6 + [shape_of((NH, rows_len, share))],
        in_specs=[SMEM] + [VMEM] * 8 + [HBM] * 3 + [VMEM] * 4,
        out_specs=[VMEM] * 7,
        scratch_shapes=[
            pltpu.VMEM((n_share, share, wq.shape[1]), bf16),
            pltpu.VMEM((n_share, share, 2 * wkv.shape[2]), bf16),
            pltpu.VMEM(wo.shape, bf16),
            pltpu.SemaphoreType.DMA((2, n_share + 1)),
        ],
        compiler_params=params(58),
        name="attention",
    )(
        places,
        *pieces,
        wq,
        wkv.reshape(model_width, -1),
        wo,
        cosine,
        sine,
        doc_ids.reshape(rows_len, 1),
        doc_ids.reshape(1, rows_len),
    )
    partial, z_two, own_blocks = tie(list(partial), z_two, own_blocks)
    got = [send_tensor(partial[4 + k], back[k], 0) for k in range(2)]
    two = send_tensor(partial[6], 2, 0)
    z_one = send_dp(own_blocks, 3, 0, 0)
    z_three = send_dp(own_blocks, 1, 0, 0)
    got, two, z_one, z_three = tie(got, two, z_one, z_three)

    rows_z = (own_blocks, z_one, z_two, z_three)
    gate_z, up_z = [
        jnp.concatenate([row[m * capacity : (m + 1) * capacity] for row in rows_z], axis=0)
        for m in range(2)
    ]
    half = NZ * capacity // 2
    crossed = wide_sum(partial[3], *got, two[1]).astype(bf16)
    from_other = send_tensor(crossed, 0, 1)
    direct = [send_tensor(partial[1 + k], back[k], 0) for k in range(2)]
    gate_x = send_x(gate_z)
    from_other, direct, gate_x, up_z = tie(from_other, direct, gate_x, up_z)

    mixed = wide_sum(tokens, partial[0], *direct, two[0], from_other).astype(bf16)
    other = send_tensor(mixed, 0, 1)
    across = [send_tensor(mixed, d, 0) for d in steps[:2]]
    up_x = send_x(up_z)
    other, across, up_x = tie(other, across, up_x)

    two = send_tensor(jnp.stack([mixed, other]), 2, 0)
    mid = [mixed, *across, two[0], other, *[send_tensor(other, d, 0) for d in steps[:2]], two[1]]
    far_a = send_dp(jnp.concatenate([gate_x[0][:half], up_x[0][:half]], axis=0), 0, 1, 0)
    far_b = send_dp(jnp.concatenate([gate_x[1][half:], up_x[1][half:]], axis=0), 0, 3, 0)
    mid[5], mid[6], two, far_a, far_b = tie(mid[5], mid[6], two, far_a, far_b)
    mid[3], mid[7] = two[0], two[1]
    mine = [gate_z, up_z, *gate_x, *up_x, far_a, far_b]
    both = [jnp.concatenate(pair, axis=0) for pair in ((gate_z, up_z), gate_x, up_x)]
    swapped = [send_dp(part, 0, 0, 1) for part in (*both, far_a, far_b)]

    slots = NC * NX * NZ * capacity
    blocks = model_width // BLK
    scratch = [
        pltpu.VMEM((slots + 1, BLK, BLK), bf16),
        pltpu.SemaphoreType.DMA((len(mine),)),
    ]
    x_b, x_t, scale, sums = pl.pallas_call(
        first_kernel,
        out_shape=[
            shape_of((blocks, rows_len, BLK)),
            shape_of((blocks, BLK, rows_len)),
            shape_of((rows_len, BLK), jnp.float32),
            shape_of((2, width, rows_len, BLK), jnp.float32),
        ],
        in_specs=[SMEM] * 4 + [VMEM] * 8 + [HBM] * len(mine),
        out_specs=[VMEM] * 4,
        scratch_shapes=scratch,
        compiler_params=params(40),
        name="first",
    )(places, list_row[0], list_place[0], col_count[0], *mid, *mine)
    hidden, d_gate, d_up = pl.pallas_call(
        second_kernel,
        out_shape=[
            shape_of((rows_len, width * BLK)),
            shape_of((width + 1, rows_len, BLK)),
            shape_of((width + 1, rows_len, BLK)),
        ],
        in_specs=[SMEM] * 3 + [VMEM] * 4 + [HBM] * len(swapped),
        out_specs=[VMEM] * 3,
        scratch_shapes=scratch,
        compiler_params=params(40),
        name="second",
    )(list_row[1], list_place[1], col_count[1], x_b, scale, sums, hidden_cot, *swapped)

    side = slots // NC
    quarter = side // NX
    half = quarter // 2

    def far(m, grads):
        kernel = lambda *refs: far_kernel(side, 12, *refs)
        return pl.pallas_call(
            kernel,
            out_shape=shape_of((side, BLK, BLK)),
            in_specs=[SMEM] * 2 + [VMEM] * 2,
            out_specs=VMEM,
            compiler_params=params(16),
            name="far",
        )(tables[m][0], tables[m][1], x_t, grads)

    gate_segments = (
        ((2 * quarter, half), (quarter + half, half)),
        ((2 * quarter + half, half), (3 * quarter, half)),
        ((quarter, half),),
        ((3 * quarter + half, half),),
        ((0, quarter),),
    )
    up_segments = (
        ((2 * quarter, half),),
        ((2 * quarter + half, half),),
        ((quarter, quarter),),
        ((3 * quarter, quarter),),
        ((0, quarter),),
    )

    def near(m, grads, add, segments):
        sizes = [sum(size for _, size in pieces) for pieces in segments]
        kernel = lambda *refs: near_kernel(12, segments, *refs)
        return pl.pallas_call(
            kernel,
            out_shape=[shape_of((size, BLK, BLK)) for size in sizes],
            in_specs=[SMEM] * 2 + [VMEM] * 3,
            out_specs=[VMEM] * len(sizes),
            compiler_params=params(16),
            name="near",
        )(tables[m][0], tables[m][1], x_t, grads, add)

    def send_first(sums):
        return send_dp(sums[0], 0, 1, 0), send_dp(sums[1], 0, 3, 0)

    def send_second(sums, left, right):
        from_left = send_dp(wide_sum(sums[2], left[:half]).astype(bf16), 0, 1, 0)
        from_right = send_dp(wide_sum(sums[3], right[:half]).astype(bf16), 0, 3, 0)
        return left, right, from_left, from_right

    def send_z(total):
        by_z = [total[d * capacity : (d + 1) * capacity] for d in range(NZ)]
        return [by_z[0]] + [send_dp(by_z[d].astype(bf16), d, 0, 0) for d in (1, 2, 3)]

    def finish(terms):
        return wide_sum(*terms).reshape(1, 1, capacity, BLK, BLK)

    far_gate = far(0, d_gate)
    swap_gate = send_dp(far_gate, 0, 0, 1)
    far_up = far(1, d_up)
    swap_up = send_dp(far_up, 0, 0, 1)
    gate_sums = near(0, d_gate, swap_gate, gate_segments)
    up_sums = list(near(1, d_up, swap_up, up_segments))
    first, up_sums = tie(send_first(gate_sums), up_sums)
    got = send_second(gate_sums, *first)
    via = send_first(up_sums)
    got, via, up_sums = tie(got, via, up_sums)
    left, right, from_left, from_right = got
    gate_total = jnp.concatenate(
        [
            wide_sum(gate_sums[4][:half], from_left, right[half:]),
            wide_sum(gate_sums[4][half:], from_right, left[half:]),
        ],
        axis=0,
    )
    gate_terms = send_z(gate_total)
    _, _, s1, s3, s0 = up_sums
    to_right = jnp.concatenate([wide_sum(s1[:half], via[0]).astype(bf16), s1[half:]], axis=0)
    to_left = jnp.concatenate([s3[:half], wide_sum(s3[half:], via[1]).astype(bf16)], axis=0)
    beside = send_first((to_right, to_left))
    gate_terms, beside = tie(gate_terms, beside)
    gate_grad = finish(gate_terms)
    up_grad = finish(send_z(wide_sum(s0, *beside)))
    return (mixed, hidden, gate_grad, up_grad)


def solution(mesh):
    in_specs = (
        P("dp", "tensor"),
        P("dp", None),
        P(None, "tensor"),
        P(None, None, "tensor"),
        P("tensor", None),
        P("dp", "tensor", None, None, None),
        P("dp", "tensor", None, None, None),
        P(),
        P(),
        P("dp", "tensor"),
    )
    out_specs = (
        P("dp", "tensor"),
        P("dp", "tensor"),
        P("dp", "tensor", None, None, None),
        P("dp", "tensor", None, None, None),
    )
    return jax.shard_map(local, mesh=mesh, in_specs=in_specs, out_specs=out_specs, check_vma=False)
```
